128 devices in a mesh: head: 4 (over x), seq: 32 (over y, z, core).
Axes of the slice: x: 4, y: 4, z: 4, core: 2. Of those that a mesh axis runs over, the one named last changes fastest.
Arguments:
- queries: bfloat16 [16384, 8192], P('seq', 'head'), may hold values from -200 to 200
- keys: bfloat16 [16384, 8192], P('seq', 'head'), may hold values from -6 to 6
- values: bfloat16 [16384, 8192], P('seq', 'head'), may hold values from -6 to 6
- cotangent: bfloat16 [16384, 8192], P('seq', 'head'), may hold values from -6 to 6
- prefix_keys: bfloat16 [16384, 8192], P('seq', 'head'), may hold values from -1.5 to 1.5
- prefix_values: bfloat16 [16384, 8192], P('seq', 'head'), may hold values from -1.5 to 1.5
- gain: float32 [8192], P('head'), may hold values from 0.5 to 1.5
- lengths: int32 [32], P('seq'), may hold values from 64 to 512, as said below
Outputs:
- normed: bfloat16 [16384, 8192], P('seq', 'head')
- query_grad: bfloat16 [16384, 8192], P('seq', 'head')
- key_grad: bfloat16 [16384, 8192], P('seq', 'head')
- value_grad: bfloat16 [16384, 8192], P('seq', 'head')
- prefix_key_grad: bfloat16 [16384, 8192], P('seq', 'head')
- prefix_value_grad: bfloat16 [16384, 8192], P('seq', 'head')
The draws below stay inside these ranges and needn't reach their ends.
Inputs may be any that keep to these rules, and one draw needn't show every extreme that they name: `lengths`: one length per response; some response has exactly 512 live slots and some exactly 64.
All inputs are finite; a program needn't handle non-finite values.
Results may differ from the reference program's by a relative error of at most 0.0058.
Values sent between devices are 32-bit elements; how exact they have to be, the bound alone decides.
No kernel may reach another device: no remote copies, remote signals or barrier semaphores. Data moves between devices by JAX's collectives and lax.ppermute only.
A program may use at most 128 MiB of HBM per device.

```python
import jax
import jax.numpy as jnp
from jax import lax

H = 64
HEAD_DIM = 128
BLOCK = 256
RMAX = 512
RESP = 32
PRE = 16384
RTOK = 16384
WIDTH = 8192


def draw_queries(key, part):
    key_head, key_row, key_base = jax.random.split(key, 3)
    col_head = lax.iota(jnp.int32, WIDTH) // HEAD_DIM
    head_factor = jax.random.uniform(key_head, (H,), jnp.float32, 0.8, 1.2)
    head_scale = 10.0 ** (col_head.astype(jnp.float32) / max(H - 1, 1)) * head_factor[col_head]
    row_scale = 10.0 ** jax.random.uniform(key_row, (RTOK, 1), jnp.float32)
    base = jax.random.normal(key_base, (RTOK, WIDTH), jnp.float32)
    return jnp.clip(base * head_scale[None, :] * row_scale, -200.0, 200.0).astype(jnp.bfloat16)


def draw_lengths(key, part):
    key_len, key_shuffle = jax.random.split(key)
    drawn = jax.random.randint(key_len, (RESP,), RMAX // 8, RMAX + 1)
    shuffled = jax.random.permutation(key_shuffle, RESP)
    return drawn.at[shuffled[0]].set(RMAX).at[shuffled[1]].set(RMAX // 8)


def block_scale(key, extent, cuts, low, high):
    loudness = 1.0
    for position, blocks in cuts:
        steps = jax.random.uniform(jax.random.fold_in(jax.random.fold_in(key, 6), position), (blocks,), jnp.float32, low / len(cuts), high / len(cuts))
        loudness = loudness * jnp.repeat(jnp.exp(steps), extent[position] // blocks).reshape((-1,) + (1,) * (len(extent) - 1 - position))
    return loudness


def gaussian(stream_key, dims, scale, reach, shards=(), dtype=jnp.bfloat16):
    level = block_scale(stream_key, dims, shards, -0.22, 0.18) if shards else 1.0
    result = jax.random.normal(stream_key, dims, jnp.float32) * scale * level
    return jnp.minimum(jnp.maximum(result, -reach), reach).astype(dtype)


def setup_inputs(seed: int = 0) -> dict:
    streams_of = jax.random.split(jax.random.key(seed), 9)
    return {
        "queries": draw_queries(jax.random.fold_in(streams_of[8], 71), 0),
        "keys": gaussian(streams_of[1], (RTOK, WIDTH), 1.0, 6.0, ((0, 32), (1, 4))),
        "values": gaussian(streams_of[2], (RTOK, WIDTH), 1.0, 6.0, ((0, 32), (1, 4))),
        "cotangent": gaussian(streams_of[3], (RTOK, WIDTH), 1.0, 6.0, ((0, 32), (1, 4))),
        "prefix_keys": gaussian(streams_of[4], (PRE, WIDTH), 0.25, 1.5, ((0, 32), (1, 4))),
        "prefix_values": gaussian(streams_of[5], (PRE, WIDTH), 0.25, 1.5, ((0, 32), (1, 4))),
        "gain": jnp.clip(1.0 + 0.1 * jax.random.normal(streams_of[6], (WIDTH,), jnp.float32), 0.5, 1.5),
        "lengths": draw_lengths(jax.random.fold_in(streams_of[8], 71), 0),
    }


epsilon = 1e-06

def rounded(value):
    return lax.optimization_barrier(value.astype(jnp.bfloat16)).astype(jnp.float32)

def reference(queries, keys, values, cotangent, prefix_keys, prefix_values, gain, lengths):
    pre_keys = prefix_keys.astype(jnp.float32).reshape(PRE, H, HEAD_DIM)
    pre_values = prefix_values.astype(jnp.float32).reshape(PRE, H, HEAD_DIM)
    prefix_state = jnp.einsum('thd,the->hde', pre_keys, pre_values)
    causal = jnp.tril(jnp.ones((BLOCK, BLOCK), jnp.float32))
    block_count = RMAX // BLOCK

    def respond(pieces):
        q_in, k_in, v_in, cot_in, length = pieces
        live_mask = (jnp.arange(RMAX) < length).astype(jnp.bfloat16)[:, None]

        def shaped(array):
            return (array * live_mask).astype(jnp.float32).reshape(block_count, BLOCK, H, HEAD_DIM)
        q_live = shaped(q_in)
        k_live = shaped(k_in)
        v_live = shaped(v_in)

        def forward(state_now, blocks):
            q_block, k_block, v_block = blocks
            state_bf = rounded(state_now)
            from_state = jnp.einsum('bhd,hde->bhe', q_block, state_bf)
            scores = rounded(jnp.einsum('bhd,shd->hbs', q_block, k_block) * causal)
            in_block = jnp.einsum('hbs,she->bhe', scores, v_block)
            state_next = state_now + jnp.einsum('bhd,bhe->hde', k_block, v_block)
            return (state_next, (from_state + in_block, scores, state_bf))
        final_state, (attended, scores_all, states_all) = lax.scan(forward, prefix_state, (q_live, k_live, v_live))
        attended = attended.reshape(RMAX, WIDTH)
        root_mean = jnp.sqrt(lax.optimization_barrier(jnp.sum(attended * attended, axis=1)) / WIDTH + epsilon)[:, None]
        normed = (gain * attended / root_mean).astype(jnp.bfloat16)
        scaled_cot = gain * (cot_in * live_mask).astype(jnp.float32)
        inner_sum = lax.optimization_barrier(jnp.sum(scaled_cot * attended, axis=1))[:, None]
        out_grad = rounded(scaled_cot / root_mean - attended * inner_sum / (WIDTH * root_mean ** 3))
        out_grad = out_grad.reshape(block_count, BLOCK, H, HEAD_DIM)

        def backward(grad_state, blocks):
            q_block, k_block, v_block, d_block, scores, state_bf = blocks
            grad_bf = rounded(grad_state)
            pscore = rounded(jnp.einsum('bhe,she->hbs', d_block, v_block) * causal)
            grad_q = jnp.einsum('bhe,hde->bhd', d_block, state_bf) + jnp.einsum('hbs,shd->bhd', pscore, k_block)
            grad_k = jnp.einsum('bhe,hde->bhd', v_block, grad_bf) + jnp.einsum('hbs,bhd->shd', pscore, q_block)
            grad_v = jnp.einsum('bhd,hde->bhe', k_block, grad_bf) + jnp.einsum('hbs,bhe->she', scores, d_block)
            grad_next = grad_state + jnp.einsum('bhd,bhe->hde', q_block, d_block)
            return (grad_next, (grad_q, grad_k, grad_v))
        grad_zero = jnp.zeros((H, HEAD_DIM, HEAD_DIM), jnp.float32)
        grad_total, (grad_q, grad_k, grad_v) = lax.scan(backward, grad_zero, (q_live, k_live, v_live, out_grad, scores_all, states_all), reverse=True)
        flat = (normed, grad_q.reshape(RMAX, WIDTH).astype(jnp.bfloat16), grad_k.reshape(RMAX, WIDTH).astype(jnp.bfloat16), grad_v.reshape(RMAX, WIDTH).astype(jnp.bfloat16))
        return (flat, grad_total)
    (normed, query_grad, key_grad, value_grad), state_grads = lax.map(respond, (queries.reshape(RESP, RMAX, WIDTH), keys.reshape(RESP, RMAX, WIDTH), values.reshape(RESP, RMAX, WIDTH), cotangent.reshape(RESP, RMAX, WIDTH), lengths))
    state_grad = lax.optimization_barrier(jnp.sum(state_grads, axis=0))
    prefix_key_grad = jnp.einsum('the,hde->thd', pre_values, state_grad, precision=lax.Precision.HIGHEST).reshape(PRE, WIDTH).astype(jnp.bfloat16)
    prefix_value_grad = jnp.einsum('thd,hde->the', pre_keys, state_grad, precision=lax.Precision.HIGHEST).reshape(PRE, WIDTH).astype(jnp.bfloat16)
    return (normed.reshape(RTOK, WIDTH), query_grad.reshape(RTOK, WIDTH), key_grad.reshape(RTOK, WIDTH), value_grad.reshape(RTOK, WIDTH), prefix_key_grad, prefix_value_grad)
```

```python
import functools

import jax
import jax.numpy as jnp
from jax import lax
from jax.sharding import PartitionSpec as P

H = 64
HEAD_DIM = 128
BLOCK = 256


epsilon = 1e-06


def sum_over_seq(part):
    seq_size = lax.axis_size("seq")
    chips = seq_size // 2
    half = part.shape[0] // 2
    core = lax.axis_index("seq") % 2
    swap = [(i, i ^ 1) for i in range(seq_size)]
    groups = [list(range(c, seq_size, 2)) for c in range(2)]
    mine = lax.dynamic_slice_in_dim(part, core * half, half, 0)
    theirs = lax.dynamic_slice_in_dim(part, (1 - core) * half, half, 0)
    paired = mine + lax.ppermute(theirs, "seq", swap)
    pieces = lax.all_to_all(
        paired.reshape(chips, -1, HEAD_DIM), "seq", 0, 0, axis_index_groups=groups, tiled=True
    )
    piece = jnp.sum(pieces, axis=0)
    gathered = lax.all_to_all(
        jnp.broadcast_to(piece[None], pieces.shape), "seq", 0, 0, axis_index_groups=groups, tiled=True
    ).reshape(mine.shape)
    other = lax.ppermute(gathered, "seq", swap)
    first = jnp.where(core == 0, gathered, other)
    second = jnp.where(core == 0, other, gathered)
    return jnp.concatenate([first, second], axis=0)


def body(queries, keys, values, cotangent, prefix_keys, prefix_values, gain, lengths):
    tok_rows, tok_cols = queries.shape
    heads_here = tok_cols // HEAD_DIM
    block_count = tok_rows // BLOCK
    length = lengths[0]
    is_live = lax.iota(jnp.int32, tok_rows) < length
    live_mask = is_live.astype(jnp.bfloat16)[:, None]
    block_shape = (block_count, BLOCK, heads_here, HEAD_DIM)
    q_live = (queries * live_mask).reshape(block_shape)
    k_live = (keys * live_mask).reshape(block_shape)
    v_live = (values * live_mask).reshape(block_shape)
    causal = (lax.iota(jnp.int32, BLOCK)[:, None] >= lax.iota(jnp.int32, BLOCK)[None, :]).astype(
        jnp.float32
    )
    pre_keys = prefix_keys.reshape(-1, heads_here, HEAD_DIM)
    pre_values = prefix_values.reshape(-1, heads_here, HEAD_DIM)
    partial_state = jnp.einsum(
        "thd,the->hde", pre_keys, pre_values, preferred_element_type=jnp.float32
    )

    def intra_block(index):
        q_block = q_live[index]
        k_block = k_live[index]
        v_block = v_live[index]
        scores = jnp.einsum("bhd,shd->hbs", q_block, k_block, preferred_element_type=jnp.float32)
        scores = (scores * causal).astype(jnp.bfloat16)
        in_block = jnp.einsum("hbs,she->bhe", scores, v_block, preferred_element_type=jnp.float32)
        block_kv = jnp.einsum("bhd,bhe->hde", k_block, v_block, preferred_element_type=jnp.float32)
        return (in_block, scores, block_kv)

    def from_state_of(index, state_bf):
        return jnp.einsum(
            "bhd,hde->bhe", q_live[index], state_bf, preferred_element_type=jnp.float32
        )

    results = []
    score_list = []
    state_list = []
    prefix_state = sum_over_seq(partial_state)

    def forward_block(index, state_now):
        state_bf = state_now.astype(jnp.bfloat16)
        in_block, scores, block_kv = intra_block(index)
        return (from_state_of(index, state_bf) + in_block, scores, state_bf, state_now + block_kv)

    state_now = prefix_state
    for index in range(block_count):
        step_fn = functools.partial(forward_block, index)
        packed = step_fn(state_now)
        results.append(packed[0])
        score_list.append(packed[1])
        state_list.append(packed[2])
        state_now = packed[3]
    attended = jnp.concatenate(results, axis=0).reshape(tok_rows, tok_cols)
    scaled_cot = gain * (cotangent * live_mask).astype(jnp.float32)
    square_sum, inner_sum = lax.psum(
        (jnp.sum(attended * attended, axis=1), jnp.sum(scaled_cot * attended, axis=1)), "head"
    )
    root_mean = jnp.sqrt(square_sum / (H * HEAD_DIM) + epsilon)[:, None]
    inner_sum = inner_sum[:, None]
    normed = (gain * attended / root_mean).astype(jnp.bfloat16)
    out_grad = scaled_cot / root_mean - attended * inner_sum / (H * HEAD_DIM * root_mean**3)
    out_grad = out_grad.astype(jnp.bfloat16).reshape(block_shape)

    def backward_block(index, grad_state):
        q_block = q_live[index]
        k_block = k_live[index]
        v_block = v_live[index]
        d_block = out_grad[index]
        scores = score_list[index]
        state_bf = state_list[index]
        grad_bf = grad_state.astype(jnp.bfloat16)
        pscore = jnp.einsum("bhe,she->hbs", d_block, v_block, preferred_element_type=jnp.float32)
        pscore = (pscore * causal).astype(jnp.bfloat16)
        grad_q = jnp.einsum(
            "bhe,hde->bhd", d_block, state_bf, preferred_element_type=jnp.float32
        ) + jnp.einsum("hbs,shd->bhd", pscore, k_block, preferred_element_type=jnp.float32)
        grad_k = jnp.einsum(
            "bhe,hde->bhd", v_block, grad_bf, preferred_element_type=jnp.float32
        ) + jnp.einsum("hbs,bhd->shd", pscore, q_block, preferred_element_type=jnp.float32)
        grad_v = jnp.einsum(
            "bhd,hde->bhe", k_block, grad_bf, preferred_element_type=jnp.float32
        ) + jnp.einsum("hbs,bhe->she", scores, d_block, preferred_element_type=jnp.float32)
        grad_next = grad_state + jnp.einsum(
            "bhd,bhe->hde", q_block, d_block, preferred_element_type=jnp.float32
        )
        return (
            grad_q.astype(jnp.bfloat16),
            grad_k.astype(jnp.bfloat16),
            grad_v.astype(jnp.bfloat16),
            grad_next,
        )

    grad_state = jnp.zeros((heads_here, HEAD_DIM, HEAD_DIM), jnp.float32)
    query_parts = []
    key_parts = []
    value_parts = []
    for index in reversed(range(block_count)):
        step_fn = functools.partial(backward_block, index)
        packed = step_fn(grad_state)
        query_parts.insert(0, packed[0])
        key_parts.insert(0, packed[1])
        value_parts.insert(0, packed[2])
        grad_state = packed[3]
    total_grad = sum_over_seq(grad_state)
    wide_keys = pre_keys.astype(jnp.float32)
    wide_values = pre_values.astype(jnp.float32)
    prefix_key_grad = jnp.einsum(
        "the,hde->thd", wide_values, total_grad, precision=lax.Precision.HIGHEST
    )
    prefix_value_grad = jnp.einsum(
        "thd,hde->the", wide_keys, total_grad, precision=lax.Precision.HIGHEST
    )
    query_grad = jnp.concatenate(query_parts, axis=0).reshape(tok_rows, tok_cols)
    key_grad = jnp.concatenate(key_parts, axis=0).reshape(tok_rows, tok_cols)
    value_grad = jnp.concatenate(value_parts, axis=0).reshape(tok_rows, tok_cols)
    return (
        normed,
        query_grad,
        key_grad,
        value_grad,
        prefix_key_grad.astype(jnp.bfloat16).reshape(prefix_keys.shape),
        prefix_value_grad.astype(jnp.bfloat16).reshape(prefix_values.shape),
    )


def solution(mesh):
    return jax.shard_map(
        body,
        mesh=mesh,
        in_specs=(
            P("seq", "head"),
            P("seq", "head"),
            P("seq", "head"),
            P("seq", "head"),
            P("seq", "head"),
            P("seq", "head"),
            P("head"),
            P("seq"),
        ),
        out_specs=(
            P("seq", "head"),
            P("seq", "head"),
            P("seq", "head"),
            P("seq", "head"),
            P("seq", "head"),
            P("seq", "head"),
        ),
        check_vma=False,
    )
```

```python
import functools

import jax
import jax.numpy as jnp
from jax import lax
from jax.experimental import pallas as pl
from jax.experimental.pallas import tpu as pltpu
from jax.sharding import PartitionSpec as P

H = 64
HEAD_DIM = 128
BLOCK = 256
WIDTH = H * HEAD_DIM
EPSILON = 1e-06

GROUP = 2
VMEM_LIMIT = 24 * 1024 * 1024

F32 = jnp.float32
BF16 = jnp.bfloat16


def dot_nn(a, b):
    return lax.dot_general(a, b, (((1,), (0,)), ((), ())), preferred_element_type=F32)


def dot_nt(a, b):
    return lax.dot_general(a, b, (((1,), (1,)), ((), ())), preferred_element_type=F32)


def dot_tn(a, b):
    return lax.dot_general(a, b, (((0,), (0,)), ((), ())), preferred_element_type=F32)


def lanes(head):
    return slice(head * HEAD_DIM, (head + 1) * HEAD_DIM)


def rows(block):
    return slice(block * BLOCK, (block + 1) * BLOCK)


def block_mask(upper):
    row = lax.broadcasted_iota(jnp.int32, (BLOCK, BLOCK), 0)
    column = lax.broadcasted_iota(jnp.int32, (BLOCK, BLOCK), 1)
    return column >= row if upper else row >= column


def prefix_state_kernel(meta, k_ref, v_ref, s_ref):
    for h in range(GROUP):
        s_ref[h] = dot_tn(k_ref[:, lanes(h)], v_ref[:, lanes(h)])


def intra_kernel(meta, q_ref, k_ref, v_ref, o_ref, kv_ref, qt_ref):
    lower = block_mask(False)
    for h in range(GROUP):
        for b in range(q_ref.shape[0] // BLOCK):
            q, k, v = (ref[rows(b), lanes(h)] for ref in (q_ref, k_ref, v_ref))
            scores = jnp.where(lower, dot_nt(q, k), 0.0).astype(BF16)
            o_ref[rows(b), lanes(h)] = dot_nn(scores, v)
        kv_ref[h] = dot_tn(k_ref[rows(0), lanes(h)], v_ref[rows(0), lanes(h)])
        qt_ref[h] = q_ref[:, lanes(h)].T


def spread_sum_kernel(pieces_ref, out_ref):
    total = jnp.sum(pieces_ref[...], axis=0)
    for i in range(out_ref.shape[0]):
        out_ref[i] = total


def forward_kernel(meta, q_ref, intra_ref, s_ref, kv_ref, dy_ref, gain_ref, *rest):
    *before, o_ref, m_ref, stats_ref, square_acc, inner_acc = rest

    @pl.when(pl.program_id(0) == 0)
    def _():
        square_acc[...] = jnp.zeros_like(square_acc)
        inner_acc[...] = jnp.zeros_like(inner_acc)

    for h in range(GROUP):
        state = s_ref[h]
        gain = gain_ref[:, lanes(h)]
        for b, m in enumerate((state.astype(BF16), (state + kv_ref[h]).astype(BF16))):
            m_ref[h, b] = m
            o = intra_ref[rows(b), lanes(h)] + dot_nn(q_ref[rows(b), lanes(h)], m)
            o_ref[rows(b), lanes(h)] = o
            square_acc[rows(b)] += o * o
            inner_acc[rows(b)] += gain * dy_ref[rows(b), lanes(h)].astype(F32) * o

    @pl.when(pl.program_id(0) == pl.num_programs(0) - 1)
    def _():
        for i, acc in enumerate((square_acc, inner_acc)):
            row = jnp.sum(acc[...].T, axis=0, keepdims=True)
            if before:
                row = row + before[0][i : i + 1]
            stats_ref[i : i + 1] = row


def out_grad(dy_ref, o_ref, gain_ref, inv_ref, coef_ref, h):
    scaled = gain_ref[:, lanes(h)] * dy_ref[:, lanes(h)].astype(F32)
    return (scaled * inv_ref[...] - o_ref[:, lanes(h)] * coef_ref[...]).astype(BF16)


def state_grad_kernel(first, meta, dy_ref, o_ref, gain_ref, qt_ref, *rest):
    if first:
        *stats, ds_ref, g_ref, inv_ref, coef_ref = rest

        @pl.when(pl.program_id(0) == 0)
        def _():
            total = sum(ref[...] for ref in stats[1:]) + stats[0][...]
            inv = 1.0 / jnp.sqrt(total[0:1] / WIDTH + EPSILON)
            coef = total[1:2] * (inv * inv * inv) / WIDTH
            live = lax.broadcasted_iota(jnp.int32, inv.shape, 1) < meta[1]
            for value, ref in ((inv, inv_ref), (coef, coef_ref)):
                value = jnp.where(live, value, 0.0)
                for n in range(value.shape[1] // HEAD_DIM):
                    square = jnp.broadcast_to(value[:, lanes(n)], (HEAD_DIM, HEAD_DIM))
                    ref[n * HEAD_DIM : (n + 1) * HEAD_DIM] = square.T

    else:
        inv_ref, coef_ref, ds_ref, g_ref = rest
    for h in range(GROUP):
        do = out_grad(dy_ref, o_ref, gain_ref, inv_ref, coef_ref, h)
        later = dot_nn(qt_ref[h][:, rows(1)], do[rows(1)])
        ds_ref[h] = later + dot_nn(qt_ref[h][:, rows(0)], do[rows(0)])
        g_ref[h] = later.astype(BF16)


def backward_kernel(
    meta, q_ref, k_ref, v_ref, dy_ref, o_ref, gain_ref, m_ref, g_ref, inv_ref, coef_ref, *rest
):
    normed_ref, dq_ref, dk_ref, dv_ref = rest[-4:]
    lower, upper = block_mask(False), block_mask(True)
    for h in range(GROUP):
        normed_ref[:, lanes(h)] = (
            gain_ref[:, lanes(h)] * o_ref[:, lanes(h)] * inv_ref[...]
        ).astype(BF16)
        do_all = out_grad(dy_ref, o_ref, gain_ref, inv_ref, coef_ref, h)
        for b in range(2):
            q, k, v = (ref[rows(b), lanes(h)] for ref in (q_ref, k_ref, v_ref))
            do = do_all[rows(b)]
            p = jnp.where(lower, dot_nt(do, v), 0.0).astype(BF16)
            p_t = jnp.where(upper, dot_nt(v, do), 0.0).astype(BF16)
            scores_t = jnp.where(upper, dot_nt(k, q), 0.0).astype(BF16)
            dq = dot_nt(do, m_ref[h, b]) + dot_nn(p, k)
            dk = dot_nn(p_t, q)
            dv = dot_nn(scores_t, do)
            if b == 0:
                dk = dk + dot_nt(v, g_ref[h])
                dv = dv + dot_nn(k, g_ref[h])
            dq_ref[rows(b), lanes(h)] = dq.astype(BF16)
            dk_ref[rows(b), lanes(h)] = dk.astype(BF16)
            dv_ref[rows(b), lanes(h)] = dv.astype(BF16)


def prefix_grad_kernel(meta, k_ref, v_ref, ds_ref, *rest):
    dk_ref, dv_ref = rest[-2:]
    for h in range(GROUP):
        ds = ds_ref[h]
        high = ds.astype(BF16)
        low = (ds - high.astype(F32)).astype(BF16)
        k, v = k_ref[:, lanes(h)], v_ref[:, lanes(h)]
        dk = dot_nt(jnp.concatenate([v, v], 1), jnp.concatenate([high, low], 1))
        dv = dot_nn(jnp.concatenate([k, k], 1), jnp.concatenate([high, low], 0))
        dk_ref[:, lanes(h)] = dk.astype(BF16)
        dv_ref[:, lanes(h)] = dv.astype(BF16)


def body(queries, keys, values, cotangent, prefix_keys, prefix_values, gain, lengths):
    tok_rows, tok_cols = queries.shape
    pre_rows = prefix_keys.shape[0]
    half = tok_cols // HEAD_DIM // 2
    steps = half // GROUP
    seq_size = lax.axis_size("seq")
    head_size = lax.axis_size("head")
    chips = seq_size // 2
    core = lax.axis_index("seq") % 2
    swap = [(i, i ^ 1) for i in range(seq_size)]
    chip_groups = [list(range(c, seq_size, 2)) for c in range(2)]
    meta = jnp.stack([core.astype(jnp.int32), lengths[0]])
    gain_row = gain[None]
    OWN, OTHER = 0, steps

    def call(kernel, part, ins, outs, flops, scratch=(), aliased=()):
        def column(i, meta):
            return (0, lax.rem(meta[0] * steps + part + i, 2 * steps))

        def spec(kind, shape):
            if kind == "wide":
                return pl.BlockSpec((shape[0], GROUP * HEAD_DIM), column)
            if kind == "half":
                return pl.BlockSpec((shape[0], GROUP * HEAD_DIM), lambda i, meta: (0, i))
            if kind == "heads":
                return pl.BlockSpec(
                    (GROUP,) + shape[1:], lambda i, meta: (i,) + (0,) * (len(shape) - 1)
                )
            return pl.BlockSpec(shape, lambda i, meta: (0,) * len(shape))

        arrays = [a for _, a in ins]
        moved = sum(a.size * a.dtype.itemsize for a in arrays) + sum(
            functools.reduce(lambda x, y: x * y, s) * jnp.dtype(d).itemsize for _, s, d in outs
        )
        return pl.pallas_call(
            kernel,
            grid_spec=pltpu.PrefetchScalarGridSpec(
                num_scalar_prefetch=1,
                grid=(steps,),
                in_specs=[spec(kind, a.shape) for kind, a in ins]
                + [pl.BlockSpec(memory_space=pl.ANY) for _ in aliased],
                out_specs=[spec(kind, s) for kind, s, _ in outs],
                scratch_shapes=scratch,
            ),
            out_shape=[jax.ShapeDtypeStruct(s, d) for _, s, d in outs],
            input_output_aliases={1 + len(arrays) + i: i for i in range(len(aliased))},
            cost_estimate=pl.CostEstimate(flops=flops, bytes_accessed=moved, transcendentals=0),
            compiler_params=pltpu.CompilerParams(vmem_limit_bytes=VMEM_LIMIT),
        )(meta, *arrays, *aliased)

    square = HEAD_DIM * HEAD_DIM
    states = (half, HEAD_DIM, HEAD_DIM)
    wide, narrow = (tok_rows, tok_cols), (tok_rows, tok_cols // 2)
    unit = 2 * half * tok_rows * square

    def exchange(value):
        return lax.all_to_all(
            value, "seq", 0, 0, axis_index_groups=chip_groups, tiled=True
        )

    def spread_sum(pieces):
        return pl.pallas_call(
            spread_sum_kernel,
            out_shape=jax.ShapeDtypeStruct(pieces.shape, F32),
            compiler_params=pltpu.CompilerParams(vmem_limit_bytes=VMEM_LIMIT),
        )(pieces)

    def sum_over_seq(mine, theirs):
        paired = mine + lax.ppermute(theirs, "seq", swap)
        pieces = exchange(paired.reshape(chips, -1, HEAD_DIM))
        gathered = exchange(spread_sum(pieces)).reshape(states)
        return gathered, lax.ppermute(gathered, "seq", swap)

    def prefix_state(part):
        return call(
            prefix_state_kernel,
            part,
            [("wide", prefix_keys), ("wide", prefix_values)],
            [("heads", states, F32)],
            unit,
        )[0]

    theirs = prefix_state(OTHER)
    mine = prefix_state(OWN)
    sums = sum_over_seq(mine, theirs)

    intra = [
        call(
            intra_kernel,
            part,
            [("wide", queries), ("wide", keys), ("wide", values)],
            [
                ("half", narrow, F32),
                ("heads", states, F32),
                ("heads", (half, HEAD_DIM, tok_rows), BF16),
            ],
            9 * unit // 2,
        )
        for part in (OWN, OTHER)
    ]

    forward = []
    for i, part in enumerate((OWN, OTHER)):
        forward.append(
            call(
                forward_kernel,
                part,
                [
                    ("wide", queries),
                    ("half", intra[i][0]),
                    ("heads", sums[i]),
                    ("heads", intra[i][1]),
                    ("wide", cotangent),
                    ("wide", gain_row),
                ]
                + [("whole", f[2]) for f in forward],
                [
                    ("half", narrow, F32),
                    ("heads", (half, 2, HEAD_DIM, HEAD_DIM), BF16),
                    ("whole", (2, tok_rows), F32),
                ],
                unit,
                scratch=[pltpu.VMEM((tok_rows, HEAD_DIM), F32)] * 2,
            )
        )
    stats = forward[1][2]
    all_stats = [stats] + [
        lax.ppermute(stats, "head", [(i, (i + k) % head_size) for i in range(head_size)])
        for k in range(1, head_size)
    ]

    def state_grad(i, part, scalars):
        first = len(scalars) > 2
        scalar = (tok_rows, HEAD_DIM)
        return call(
            functools.partial(state_grad_kernel, first),
            part,
            [
                ("wide", cotangent),
                ("half", forward[i][0]),
                ("wide", gain_row),
                ("heads", intra[i][2]),
            ]
            + [("whole", a) for a in scalars],
            [("heads", states, F32), ("heads", states, BF16)]
            + [("whole", scalar, F32), ("whole", scalar, F32)] * first,
            unit,
        )

    theirs, later_other, inv, coef = state_grad(1, OTHER, all_stats)
    mine, later_own = state_grad(0, OWN, [inv, coef])
    sums = sum_over_seq(mine, theirs)

    grads = ()
    for i, (part, later) in enumerate(((OWN, later_own), (OTHER, later_other))):
        grads = call(
            backward_kernel,
            part,
            [
                ("wide", queries),
                ("wide", keys),
                ("wide", values),
                ("wide", cotangent),
                ("half", forward[i][0]),
                ("wide", gain_row),
                ("heads", forward[i][1]),
                ("heads", later),
                ("whole", inv),
                ("whole", coef),
            ],
            [("wide", wide, BF16)] * 4,
            16 * unit,
            aliased=grads,
        )

    prefix_grads = ()
    for part, total in ((OWN, sums[0]), (OTHER, sums[1])):
        prefix_grads = call(
            prefix_grad_kernel,
            part,
            [("wide", prefix_keys), ("wide", prefix_values), ("heads", total)],
            [("wide", (pre_rows, tok_cols), BF16)] * 2,
            4 * unit,
            aliased=prefix_grads,
        )
    return (*grads, *prefix_grads)


def solution(mesh):
    spread = P("seq", "head")
    return jax.shard_map(
        body,
        mesh=mesh,
        in_specs=(spread,) * 6 + (P("head"), P("seq")),
        out_specs=(spread,) * 6,
        check_vma=False,
    )
```

```python
import functools

import jax
import jax.numpy as jnp
from jax import lax
from jax.experimental import pallas as pl
from jax.experimental.pallas import tpu as pltpu
from jax.sharding import PartitionSpec as P

H = 64
HEAD_DIM = 128
BLOCK = 256
WIDTH = H * HEAD_DIM
EPSILON = 1e-06

GROUP = 2
SLAB = GROUP * HEAD_DIM
MIB = 1024 * 1024

F32 = jnp.float32
BF16 = jnp.bfloat16


def dot_nn(a, b):
    return lax.dot_general(a, b, (((1,), (0,)), ((), ())), preferred_element_type=F32)


def dot_nt(a, b):
    return lax.dot_general(a, b, (((1,), (1,)), ((), ())), preferred_element_type=F32)


def dot_tn(a, b):
    return lax.dot_general(a, b, (((0,), (0,)), ((), ())), preferred_element_type=F32)


def lanes(head):
    return slice(head * HEAD_DIM, (head + 1) * HEAD_DIM)


def rows(block):
    return slice(block * BLOCK, (block + 1) * BLOCK)


def block_mask(upper):
    row = lax.broadcasted_iota(jnp.int32, (BLOCK, BLOCK), 0)
    column = lax.broadcasted_iota(jnp.int32, (BLOCK, BLOCK), 1)
    return column >= row if upper else row >= column


class Slabs:
    def __init__(self, ref, buffers, semaphores, other, out=False):
        core = lax.axis_index("seq") % 2
        self.half = 1 - core if other else core
        self.ref, self.buffers, self.semaphores, self.out = ref, buffers, semaphores, out

    def copy(self, g):
        if len(self.ref.shape) == 2:
            start = pl.multiple_of(self.half * (self.buffers.shape[0] * SLAB) + g * SLAB, SLAB)
            there = self.ref.at[:, pl.ds(start, SLAB)]
        else:
            there = self.ref.at[pl.ds(g * GROUP, GROUP)]
        here = self.buffers.at[g]
        source, target = (here, there) if self.out else (there, here)
        return pltpu.make_async_copy(source, target, self.semaphores.at[g])

    def __getitem__(self, index):
        return self.buffers[index]

    def __setitem__(self, index, value):
        self.buffers[index] = value


def buffer_shape(shape):
    if len(shape) == 2:
        return (shape[1] // 2 // SLAB, shape[0], SLAB)
    return (shape[0] // GROUP, GROUP) + tuple(shape[1:])


def streamed(kernel, other, half, ins, outs, late, rest, groups):
    for g in range(groups):
        for slab in ins:
            slab.copy(g).start()
    for g in range(groups):
        for slab in late:
            slab.copy(g).start()
    steps = kernel(half, ins, outs, rest)
    step = next(steps)

    def one(g, carry):
        for slab in ins:
            slab.copy(g).wait()
        step(g)
        for slab in outs:
            slab.copy(g).start()
        return carry

    lax.fori_loop(0, groups, one, 0)
    for _ in steps:
        pass
    for g in range(groups):
        for slab in (*outs, *late):
            slab.copy(g).wait()


def prefix_state_kernel(half, ins, outs, rest):
    k, v = ins
    (s_ref,) = rest

    def step(g):
        for h in range(GROUP):
            s_ref[g * GROUP + h] = dot_tn(k[g, :, lanes(h)], v[g, :, lanes(h)])

    yield step


def intra_kernel(half, ins, outs, rest):
    o_all, kv_all, qt_all = outs
    lower = block_mask(False)

    def step(g):
        for h in range(GROUP):
            for b in range(2):
                q, k, v = (slab[g, rows(b), lanes(h)] for slab in ins)
                scores = jnp.where(lower, dot_nt(q, k), 0.0).astype(BF16)
                o_all[g, h, rows(b)] = dot_nn(scores, v)
                if b == 0:
                    kv_all[g, h] = dot_tn(k, v)
            qt_all[g, h] = ins[0][g, :, lanes(h)].T

    yield step


def spread_sum_kernel(pieces_ref, out_ref):
    total = jnp.sum(pieces_ref[...], axis=0)
    for i in range(out_ref.shape[0]):
        out_ref[i] = total


def forward_kernel(half, ins, outs, rest):
    q, dy, intra, kv = ins
    (m_all,) = outs
    s_ref, gain_ref, *before = rest[:-4]
    o_ref, stats_ref, square_acc, inner_acc = rest[-4:]
    heads = o_ref.shape[0]
    square_acc[...] = jnp.zeros_like(square_acc)
    inner_acc[...] = jnp.zeros_like(inner_acc)

    def step(g):
        for b in range(2):
            square = inner = 0.0
            for h in range(GROUP):
                head = g * GROUP + h
                state = s_ref[head] if b == 0 else s_ref[head] + kv[g, h]
                m = state.astype(BF16)
                m_all[g, h, b] = m
                o = intra[g, h, rows(b)] + dot_nn(q[g, rows(b), lanes(h)], m)
                o_ref[head, rows(b)] = o
                gain = gain_ref[half * heads + head]
                square = square + o * o
                inner = inner + gain * dy[g, rows(b), lanes(h)].astype(F32) * o
            square_acc[rows(b)] += square
            inner_acc[rows(b)] += inner

    yield step
    for i, acc in enumerate((square_acc, inner_acc)):
        row = jnp.sum(acc[...].T, axis=0, keepdims=True)
        if before:
            row = row + before[0][i : i + 1]
        stats_ref[i : i + 1] = row


def state_grad_kernel(first, half, ins, outs, rest):
    (g_all,) = outs
    dy_ref, o_ref, gain_ref, qt_ref, *rest = rest
    if first:
        length_ref, *stats, ds_ref, inv_ref, coef_ref = rest
        total = sum(ref[...] for ref in stats[1:]) + stats[0][...]
        inv = 1.0 / jnp.sqrt(total[0:1] / WIDTH + EPSILON)
        coef = total[1:2] * (inv * inv * inv) / WIDTH
        live = lax.broadcasted_iota(jnp.int32, inv.shape, 1) < length_ref[0]
        for value, ref in ((inv, inv_ref), (coef, coef_ref)):
            value = jnp.where(live, value, 0.0)
            for n in range(value.shape[1] // HEAD_DIM):
                square = jnp.broadcast_to(value[:, lanes(n)], (HEAD_DIM, HEAD_DIM))
                ref[n * HEAD_DIM : (n + 1) * HEAD_DIM] = square.T
    else:
        inv_ref, coef_ref, ds_ref = rest
    heads = o_ref.shape[0]

    def step(g):
        for h in range(GROUP):
            head = g * GROUP + h
            scaled = gain_ref[half * heads + head] * dy_ref[g, :, lanes(h)].astype(F32)
            do = (scaled * inv_ref[...] - o_ref[head] * coef_ref[...]).astype(BF16)
            later = dot_nn(qt_ref[g, h, :, rows(1)], do[rows(1)])
            ds_ref[head] = later + dot_nn(qt_ref[g, h, :, rows(0)], do[rows(0)])
            g_all[g, h] = later.astype(BF16)

    yield step


def backward_kernel(half, ins, outs, rest):
    q_all, k_all, v_all, dy, o_all, m_all, g_all = ins
    normed, dq_all, dk_all, dv_all = outs
    gain_ref, inv_ref, coef_ref = rest[:3]
    heads = gain_ref.shape[0] // 2
    lower, upper = block_mask(False), block_mask(True)

    def step(g):
        for h in range(GROUP):
            o = o_all[g, h]
            gain = gain_ref[half * heads + g * GROUP + h]
            normed[g, :, lanes(h)] = (gain * o * inv_ref[...]).astype(BF16)
            scaled = gain * dy[g, :, lanes(h)].astype(F32)
            do_all = (scaled * inv_ref[...] - o * coef_ref[...]).astype(BF16)
            later = g_all[g, h]
            for b in range(2):
                q, k, v = (slab[g, rows(b), lanes(h)] for slab in (q_all, k_all, v_all))
                do = do_all[rows(b)]
                p = jnp.where(lower, dot_nt(do, v), 0.0).astype(BF16)
                p_t = jnp.where(upper, dot_nt(v, do), 0.0).astype(BF16)
                scores_t = jnp.where(upper, dot_nt(k, q), 0.0).astype(BF16)
                dq = dot_nt(do, m_all[g, h, b]) + dot_nn(p, k)
                dk = dot_nn(p_t, q)
                dv = dot_nn(scores_t, do)
                if b == 0:
                    dk = dk + dot_nt(v, later)
                    dv = dv + dot_nn(k, later)
                for slab, value in ((dq_all, dq), (dk_all, dk), (dv_all, dv)):
                    slab[g, rows(b), lanes(h)] = value.astype(BF16)

    yield step


def prefix_grad_kernel(half, ins, outs, rest):
    dk, dv = outs
    k_ref, v_ref, ds_ref = rest[:3]

    def step(g):
        for h in range(GROUP):
            ds = ds_ref[g * GROUP + h]
            high = ds.astype(BF16)
            low = (ds - high.astype(F32)).astype(BF16)
            k, v = k_ref[g, :, lanes(h)], v_ref[g, :, lanes(h)]
            dk[g, :, lanes(h)] = dot_nt(
                jnp.concatenate([v, v], 1), jnp.concatenate([high, low], 1)
            ).astype(BF16)
            dv[g, :, lanes(h)] = dot_nn(
                jnp.concatenate([k, k], 1), jnp.concatenate([high, low], 0)
            ).astype(BF16)

    yield step


HBM = pl.BlockSpec(memory_space=pltpu.HBM)
VMEM = pl.BlockSpec(memory_space=pltpu.VMEM)
SMEM = pl.BlockSpec(memory_space=pltpu.SMEM)


def in_hbm(array):
    return pltpu.with_memory_space_constraint(array, pltpu.HBM)


def in_vmem(array):
    return pltpu.with_memory_space_constraint(array, pltpu.VMEM)


def body(queries, keys, values, cotangent, prefix_keys, prefix_values, gain, lengths):
    tok_rows, tok_cols = queries.shape
    half = tok_cols // HEAD_DIM // 2
    seq_size = lax.axis_size("seq")
    head_size = lax.axis_size("head")
    chips = seq_size // 2
    swap = [(i, i ^ 1) for i in range(seq_size)]
    chip_groups = [list(range(c, seq_size, 2)) for c in range(2)]
    gains = gain.reshape(2 * half, 1, HEAD_DIM)
    OWN, OTHER = False, True

    def call(kernel, other, streams, held, outs, out_streams, flops, scratch=(), aliased=(), late=(), keep=()):
        n_in, n_out, n_late = len(streams), len(out_streams), len(late)
        fetched = [*streams, *(a for a, _ in late)]
        kept = [pltpu.VMEM(buffer_shape(streams[i].shape), streams[i].dtype) for i in keep]
        kept += [pltpu.VMEM(buffer_shape(a.shape), a.dtype) for a, _ in late]
        in_scratch = [i for i in range(n_in) if i not in keep]
        buffers = [pltpu.VMEM(buffer_shape(streams[i].shape), streams[i].dtype) for i in in_scratch]
        buffers += [pltpu.VMEM(buffer_shape(s), d) for s, d in out_streams]
        results = [pltpu.VMEM(s, d) for s, d in outs] + kept
        results += [pltpu.HBM(s, d) for s, d in out_streams]
        groups = half // GROUP
        size = sum(a.size * a.dtype.itemsize for a in (*fetched, *held))

        def run(*refs):
            refs = list(refs)

            def take(count):
                taken = refs[:count]
                del refs[:count]
                return taken

            sources, late_sources, held_refs, _ = (
                take(n) for n in (n_in, n_late, len(held), len(aliased))
            )
            out_refs, kept_refs, late_buffers, targets = (
                take(n) for n in (len(outs), len(keep), n_late, n_out)
            )
            scratch_refs, loose, out_buffers = (
                take(n) for n in (len(scratch), len(in_scratch), n_out)
            )
            (sems,) = refs
            in_buffers = dict(zip(keep, kept_refs)) | dict(zip(in_scratch, loose))
            ins = [Slabs(sources[i], in_buffers[i], sems.at[i], other) for i in range(n_in)]
            brought = [
                Slabs(late_sources[i], late_buffers[i], sems.at[n_in + i], late[i][1])
                for i in range(n_late)
            ]
            written = [
                Slabs(targets[i], out_buffers[i], sems.at[n_in + n_late + i], other, True)
                for i in range(n_out)
            ]
            core = lax.axis_index("seq") % 2
            rest = [*held_refs, *out_refs, *scratch_refs]
            streamed(kernel, other, 1 - core if other else core, ins, written, brought, rest, groups)

        integer = [jnp.issubdtype(a.dtype, jnp.integer) for a in held]
        first_aliased = len(fetched) + len(held)
        return pl.pallas_call(
            run,
            in_specs=[HBM] * len(fetched)
            + [SMEM if i else VMEM for i in integer]
            + [HBM] * len(aliased),
            out_specs=[VMEM] * (len(outs) + len(kept)) + [HBM] * n_out,
            out_shape=results,
            scratch_shapes=[
                *scratch,
                *buffers,
                pltpu.SemaphoreType.DMA((n_in + n_late + n_out, groups)),
            ],
            input_output_aliases={
                first_aliased + i: len(outs) + len(kept) + i for i in range(len(aliased))
            },
            cost_estimate=pl.CostEstimate(flops=flops, bytes_accessed=size, transcendentals=0),
            compiler_params=pltpu.CompilerParams(vmem_limit_bytes=VMEM_LIMIT),
        )(
            *(in_hbm(a) for a in fetched),
            *(a if i else in_vmem(a) for a, i in zip(held, integer)),
            *(in_hbm(a) for a in aliased),
        )

    square = HEAD_DIM * HEAD_DIM
    states = (half, HEAD_DIM, HEAD_DIM)
    tokens = (half, tok_rows, HEAD_DIM)
    scalar = (tok_rows, HEAD_DIM)
    unit = 2 * half * tok_rows * square

    def exchange(value):
        return lax.all_to_all(value, "seq", 0, 0, axis_index_groups=chip_groups, tiled=True)

    def spread_sum(pieces):
        return pl.pallas_call(
            spread_sum_kernel,
            in_specs=[VMEM],
            out_specs=VMEM,
            out_shape=jax.ShapeDtypeStruct(pieces.shape, F32),
            compiler_params=pltpu.CompilerParams(vmem_limit_bytes=VMEM_LIMIT),
        )(pieces)

    def sum_over_seq(mine, theirs, beside_sum, beside_gather):
        paired = mine + lax.ppermute(theirs, "seq", swap)
        pieces = exchange(paired.reshape(chips, -1, HEAD_DIM))
        pieces, first = lax.optimization_barrier((pieces, beside_sum()))
        gathered = exchange(spread_sum(pieces)).reshape(states)
        gathered, second = lax.optimization_barrier((gathered, beside_gather(first)))
        return gathered, lax.ppermute(gathered, "seq", swap), first, second

    def prefix_state(other):
        return call(
            prefix_state_kernel, other, [prefix_keys, prefix_values], [], [(states, F32)], [], unit
        )[0]

    def intra_of(other):
        outs = [(tokens, F32), (states, F32), ((half, HEAD_DIM, tok_rows), BF16)]
        return call(intra_kernel, other, [queries, keys, values], [], [], outs, 9 * unit // 2)

    theirs = prefix_state(OTHER)
    mine = prefix_state(OWN)
    *sums, intra_own, intra_other = sum_over_seq(
        mine, theirs, lambda: intra_of(OWN), lambda _: intra_of(OTHER)
    )

    forward = []
    for other, total, (o, kv, qt) in ((OWN, sums[0], intra_own), (OTHER, sums[1], intra_other)):
        forward.append(
            call(
                forward_kernel,
                other,
                [queries, cotangent, o, kv],
                [total, gains] + [f[1] for f in forward],
                [(tokens, F32), ((2, tok_rows), F32)],
                [((half, 2, HEAD_DIM, HEAD_DIM), BF16)],
                unit,
                scratch=[pltpu.VMEM(scalar, F32)] * 2,
                keep=[1],
                late=[(qt, other)],
            )
        )
    stats = forward[1][1]
    all_stats = [stats] + [
        lax.ppermute(stats, "head", [(i, (i + k) % head_size) for i in range(head_size)])
        for k in range(1, head_size)
    ]

    def state_grad(i, other, scalars):
        o, _, dy, qt, _ = forward[i]
        first = len(scalars) > 2
        outs = [(states, F32)] + [(scalar, F32), (scalar, F32)] * first
        kernel = functools.partial(state_grad_kernel, first)
        held = [dy, o, gains, qt, *scalars]
        return call(kernel, other, [], held, outs, [(states, BF16)], unit)

    theirs, inv, coef, later_other = state_grad(1, OTHER, [lengths, *all_stats])
    mine, later_own = state_grad(0, OWN, [inv, coef])

    def backward_of(i, other, later, before=(), late=()):
        o, _, _, _, m = forward[i]
        return call(
            backward_kernel,
            other,
            [queries, keys, values, cotangent, o, m, later],
            [gains, inv, coef],
            [],
            [(queries.shape, BF16)] * 4,
            16 * unit,
            aliased=before,
            late=late,
        )

    *sums, _, (pre_k, pre_v, *grads) = sum_over_seq(
        mine,
        theirs,
        lambda: backward_of(0, OWN, later_own),
        lambda before: backward_of(
            1, OTHER, later_other, before, [(prefix_keys, OWN), (prefix_values, OWN)]
        ),
    )

    def prefix_grad(other, k, v, total, before=(), late=()):
        return call(
            prefix_grad_kernel,
            other,
            [],
            [k, v, total],
            [],
            [(prefix_keys.shape, BF16)] * 2,
            4 * unit,
            aliased=before,
            late=late,
        )

    pre_k, pre_v, *prefix_grads = prefix_grad(
        OWN, pre_k, pre_v, sums[0], late=[(prefix_keys, OTHER), (prefix_values, OTHER)]
    )
    prefix_grads = prefix_grad(OTHER, pre_k, pre_v, sums[1], prefix_grads)
    return (*grads, *prefix_grads)


VMEM_LIMIT = 14 * MIB


def solution(mesh):
    spread = P("seq", "head")
    return jax.shard_map(
        body,
        mesh=mesh,
        in_specs=(spread,) * 6 + (P("head"), P("seq")),
        out_specs=(spread,) * 6,
        check_vma=False,
    )
```

```python
import functools

import jax
import jax.numpy as jnp
from jax import lax
from jax.experimental import pallas as pl
from jax.experimental.pallas import tpu as pltpu
from jax.sharding import PartitionSpec as P

H = 64
HEAD_DIM = 128
BLOCK = 256
WIDTH = H * HEAD_DIM
EPSILON = 1e-06

LARGE, SMALL = 4, 2
MIB = 1024 * 1024

F32 = jnp.float32
BF16 = jnp.bfloat16


def dot_nn(a, b):
    return lax.dot_general(a, b, (((1,), (0,)), ((), ())), preferred_element_type=F32)


def dot_nt(a, b):
    return lax.dot_general(a, b, (((1,), (1,)), ((), ())), preferred_element_type=F32)


def dot_tn(a, b):
    return lax.dot_general(a, b, (((0,), (0,)), ((), ())), preferred_element_type=F32)


def lanes(head):
    return slice(head * HEAD_DIM, (head + 1) * HEAD_DIM)


def rows(block):
    return slice(block * BLOCK, (block + 1) * BLOCK)


def block_mask(upper):
    row = lax.broadcasted_iota(jnp.int32, (BLOCK, BLOCK), 0)
    column = lax.broadcasted_iota(jnp.int32, (BLOCK, BLOCK), 1)
    return column >= row if upper else row >= column


class Slabs:
    def __init__(self, ref, buffers, semaphores, other, out=False):
        core = lax.axis_index("seq") % 2
        self.half = 1 - core if other else core
        self.ref, self.buffers, self.semaphores, self.out = ref, buffers, semaphores, out
        self.started = set()

    def copy(self, g):
        if len(self.ref.shape) == 2:
            slab = self.buffers.shape[-1]
            start = pl.multiple_of(self.half * (self.buffers.shape[0] * slab) + g * slab, slab)
            there = self.ref.at[:, pl.ds(start, slab)]
        else:
            group = self.buffers.shape[1]
            there = self.ref.at[pl.ds(g * group, group)]
        here = self.buffers.at[g]
        source, target = (here, there) if self.out else (there, here)
        return pltpu.make_async_copy(source, target, self.semaphores.at[g])

    def start(self, g):
        if g not in self.started:
            self.started.add(g)
            self.copy(g).start()

    def __getitem__(self, index):
        return self.buffers[index]

    def __setitem__(self, index, value):
        self.buffers[index] = value


class Below:
    def __init__(self, ref, first):
        self.ref, self.first = ref, first

    def __getitem__(self, index):
        return self.ref[(*index, slice(self.first, None))]

    def __setitem__(self, index, value):
        self.ref[(*index, slice(self.first, None))] = value


def buffer_shape(shape, group):
    if len(shape) == 2:
        slab = group * HEAD_DIM
        return (shape[1] // 2 // slab, shape[0], slab)
    return (shape[0] // group, group) + tuple(shape[1:])


def streamed(kernel, half, group, groups, whole, ins, outs, late, rest):
    for copy in whole:
        copy.start()
    for slabs in (ins, late):
        for g in range(max([slab.buffers.shape[0] for slab in slabs], default=0)):
            for slab in slabs:
                if g < slab.buffers.shape[0]:
                    slab.copy(g).start()
    steps = kernel(half, group, ins, outs, rest)
    step = next(steps)
    for copy in whole:
        copy.wait()
    for g in range(groups):
        for slab in ins:
            slab.copy(g).wait()
        step(g)
        for slab in outs:
            slab.start(g)
    for _ in steps:
        pass
    for slab in (*outs, *late):
        for g in range(slab.buffers.shape[0]):
            slab.copy(g).wait()


def prefix_state_kernel(half, group, ins, outs, rest):
    k, v, s_ref = (*ins, *rest)

    def step(g):
        for h in range(group):
            s_ref[g * group + h] = dot_tn(k[g, :, lanes(h)], v[g, :, lanes(h)])

    yield step


def bring_kernel(half, group, ins, outs, rest):
    yield lambda g: None


def intra_kernel(half, group, ins, outs, rest):
    tok_rows = ins[0].buffers.shape[1]
    o_all, kv_all, qt_all = (rest[0], Below(rest[0], tok_rows), *outs) if rest else outs
    lower = block_mask(False)

    def step(g):
        for h in range(group):
            for b in range(2):
                q, k, v = (slab[g, rows(b), lanes(h)] for slab in ins)
                scores = jnp.where(lower, dot_nt(q, k), 0.0).astype(BF16)
                o_all[g, h, rows(b)] = dot_nn(scores, v)
                if b == 0:
                    kv_all[g, h] = dot_tn(k, v)
            qt_all[g, h] = ins[0][g, :, lanes(h)].T

    yield step


def spread_sum_kernel(pieces_ref, out_ref):
    total = jnp.sum(pieces_ref[...], axis=0)
    for i in range(out_ref.shape[0]):
        out_ref[i] = total


def forward_kernel(half, group, ins, outs, rest):
    (m_all,) = outs
    if ins:
        intra, s_ref, gain_ref, *before = rest[:-4]
        (q, dy), kv = ins, Below(intra, ins[0].buffers.shape[1])
    else:
        q, dy, kv, intra, s_ref, gain_ref, *before = rest[:-4]
    o_ref, stats_ref, square_acc, inner_acc = rest[-4:]
    heads = o_ref.shape[0]
    square_acc[...] = jnp.zeros_like(square_acc)
    inner_acc[...] = jnp.zeros_like(inner_acc)

    def step(g):
        for b in range(2):
            square = inner = 0.0
            for h in range(group):
                head = g * group + h
                state = s_ref[head] if b == 0 else s_ref[head] + kv[g, h]
                m = state.astype(BF16)
                m_all[g, h, b] = m
                o = intra[g, h, rows(b)] + dot_nn(q[g, rows(b), lanes(h)], m)
                o_ref[head, rows(b)] = o
                gain = gain_ref[half * heads + head]
                square = square + o * o
                inner = inner + gain * dy[g, rows(b), lanes(h)].astype(F32) * o
            square_acc[rows(b)] += square
            inner_acc[rows(b)] += inner

    yield step
    for i, acc in enumerate((square_acc, inner_acc)):
        row = jnp.sum(acc[...].T, axis=0, keepdims=True)
        if before:
            row = row + before[0][i : i + 1]
        stats_ref[i : i + 1] = row


def state_grad_kernel(first, half, group, ins, outs, rest):
    (g_all,) = outs
    dy_ref, o_ref, gain_ref, qt_ref, *rest = rest
    if first:
        length_ref, *stats, ds_ref, inv_ref, coef_ref = rest
        total = sum(ref[...] for ref in stats[1:]) + stats[0][...]
        inv = 1.0 / jnp.sqrt(total[0:1] / WIDTH + EPSILON)
        coef = total[1:2] * (inv * inv * inv) / WIDTH
        live = lax.broadcasted_iota(jnp.int32, inv.shape, 1) < length_ref[0]
        for value, ref in ((inv, inv_ref), (coef, coef_ref)):
            value = jnp.where(live, value, 0.0)
            for n in range(value.shape[1] // HEAD_DIM):
                square = jnp.broadcast_to(value[:, lanes(n)], (HEAD_DIM, HEAD_DIM))
                ref[n * HEAD_DIM : (n + 1) * HEAD_DIM] = square.T
    else:
        inv_ref, coef_ref, ds_ref = rest
    heads = o_ref.shape[0]

    def step(g):
        for h in range(group):
            head = g * group + h
            scaled = gain_ref[half * heads + head] * dy_ref[g, :, lanes(h)].astype(F32)
            do = (scaled * inv_ref[...] - o_ref[head] * coef_ref[...]).astype(BF16)
            later = dot_nn(qt_ref[g, h, :, rows(1)], do[rows(1)])
            ds_ref[head] = later + dot_nn(qt_ref[g, h, :, rows(0)], do[rows(0)])
            g_all[g, h] = later.astype(BF16)

    yield step


def backward_kernel(half, group, ins, outs, rest):
    q_all, k_all, v_all, dy, o_all, m_all, g_all = ins
    normed, dq_all, dk_all, dv_all = outs
    gain_ref, inv_ref, coef_ref = rest
    heads = gain_ref.shape[0] // 2
    lower, upper = block_mask(False), block_mask(True)

    def step(g):
        for h in range(group):
            o = o_all[g, h]
            gain = gain_ref[half * heads + g * group + h]
            normed[g, :, lanes(h)] = (gain * o * inv_ref[...]).astype(BF16)
            scaled = gain * dy[g, :, lanes(h)].astype(F32)
            do_all = (scaled * inv_ref[...] - o * coef_ref[...]).astype(BF16)
            later = g_all[g, h]
            for b in range(2):
                q, k, v = (slab[g, rows(b), lanes(h)] for slab in (q_all, k_all, v_all))
                do = do_all[rows(b)]
                p = jnp.where(lower, dot_nt(do, v), 0.0).astype(BF16)
                p_t = jnp.where(upper, dot_nt(v, do), 0.0).astype(BF16)
                scores_t = jnp.where(upper, dot_nt(k, q), 0.0).astype(BF16)
                dq = dot_nt(do, m_all[g, h, b]) + dot_nn(p, k)
                dk = dot_nn(p_t, q)
                dv = dot_nn(scores_t, do)
                if b == 0:
                    dk = dk + dot_nt(v, later)
                    dv = dv + dot_nn(k, later)
                for slab, value in ((dq_all, dq), (dk_all, dk), (dv_all, dv)):
                    slab[g, rows(b), lanes(h)] = value.astype(BF16)

    yield step


def prefix_grad_kernel(half, group, ins, outs, rest):
    dk, dv = outs
    k, ds_ref, v = (*rest, *ins)

    def split(head):
        ds = ds_ref[head]
        high = ds.astype(BF16)
        return high, (ds - high.astype(F32)).astype(BF16)

    def value_grad(g):
        for h in range(group):
            part = k[g, :, lanes(h)]
            both = jnp.concatenate(split(g * group + h), 0)
            dv[g, :, lanes(h)] = dot_nn(jnp.concatenate([part, part], 1), both).astype(BF16)

    def key_grad(g):
        for h in range(group):
            part = v[g, :, lanes(h)]
            both = jnp.concatenate(split(g * group + h), 1)
            dk[g, :, lanes(h)] = dot_nt(jnp.concatenate([part, part], 1), both).astype(BF16)

    if ins:
        for g in range(rest[0].shape[0]):
            value_grad(g)
            dv.start(g)
        yield key_grad
    else:

        def step(g):
            value_grad(g)
            key_grad(g)

        yield step


HBM = pl.BlockSpec(memory_space=pltpu.HBM)
VMEM = pl.BlockSpec(memory_space=pltpu.VMEM)
SMEM = pl.BlockSpec(memory_space=pltpu.SMEM)


def in_hbm(array):
    return pltpu.with_memory_space_constraint(array, pltpu.HBM)


def in_vmem(array):
    return pltpu.with_memory_space_constraint(array, pltpu.VMEM)


def body(queries, keys, values, cotangent, prefix_keys, prefix_values, gain, lengths):
    tok_rows, tok_cols = queries.shape
    half = tok_cols // HEAD_DIM // 2
    seq_size = lax.axis_size("seq")
    head_size = lax.axis_size("head")
    chips = seq_size // 2
    swap = [(i, i ^ 1) for i in range(seq_size)]
    chip_groups = [list(range(c, seq_size, 2)) for c in range(2)]
    gains = gain.reshape(2 * half, 1, HEAD_DIM)
    OWN, OTHER = False, True

    def call(kernel, other, streams, held, outs, out_streams, flops, group=LARGE, scratch=(), aliased=(), late=(), keep=(), whole=()):
        n_in, n_out, n_late = len(streams), len(out_streams), len(late)
        fetched = [*streams, *(a for a, *_ in late), *whole]
        kept = [pltpu.VMEM(buffer_shape(streams[i].shape, group), streams[i].dtype) for i in keep]
        kept += [pltpu.VMEM(buffer_shape(a.shape, n), a.dtype) for a, _, n in late]
        in_scratch = [i for i in range(n_in) if i not in keep]
        buffers = [
            pltpu.VMEM(buffer_shape(streams[i].shape, group), streams[i].dtype) for i in in_scratch
        ]
        buffers += [pltpu.VMEM(buffer_shape(s, group), d) for s, d in out_streams]
        buffers += [pltpu.VMEM(a.shape, a.dtype) for a in whole]
        results = [pltpu.VMEM(s, d) for s, d in outs] + kept
        results += [pltpu.HBM(s, d) for s, d in out_streams]
        groups = half // group
        size = sum(a.size * a.dtype.itemsize for a in (*fetched, *held))

        def run(*refs):
            refs = list(refs)

            def take(count):
                taken = refs[:count]
                del refs[:count]
                return taken

            sources, late_sources, whole_sources, held_refs, _ = (
                take(n) for n in (n_in, n_late, len(whole), len(held), len(aliased))
            )
            out_refs, kept_refs, late_buffers, targets = (
                take(n) for n in (len(outs), len(keep), n_late, n_out)
            )
            scratch_refs, loose, out_buffers, whole_refs = (
                take(n) for n in (len(scratch), len(in_scratch), n_out, len(whole))
            )
            (sems,) = refs
            copies = [
                pltpu.make_async_copy(a, b, sems.at[n_in + n_late + n_out + i, 0])
                for i, (a, b) in enumerate(zip(whole_sources, whole_refs))
            ]
            in_buffers = dict(zip(keep, kept_refs)) | dict(zip(in_scratch, loose))
            ins = [Slabs(sources[i], in_buffers[i], sems.at[i], other) for i in range(n_in)]
            brought = [
                Slabs(late_sources[i], late_buffers[i], sems.at[n_in + i], late[i][1])
                for i in range(n_late)
            ]
            written = [
                Slabs(targets[i], out_buffers[i], sems.at[n_in + n_late + i], other, True)
                for i in range(n_out)
            ]
            core = lax.axis_index("seq") % 2
            this_half = 1 - core if other else core
            rest = [*held_refs, *whole_refs, *out_refs, *scratch_refs]
            streamed(kernel, this_half, group, groups, copies, ins, written, brought, rest)

        integer = [jnp.issubdtype(a.dtype, jnp.integer) for a in held]
        first_aliased = len(fetched) + len(held)
        return pl.pallas_call(
            run,
            in_specs=[HBM] * len(fetched)
            + [SMEM if i else VMEM for i in integer]
            + [HBM] * len(aliased),
            out_specs=[VMEM] * (len(outs) + len(kept)) + [HBM] * n_out,
            out_shape=results,
            scratch_shapes=[
                *scratch,
                *buffers,
                pltpu.SemaphoreType.DMA((n_in + n_late + n_out + len(whole), half // SMALL)),
            ],
            input_output_aliases={
                first_aliased + i: len(outs) + len(kept) + i for i in range(len(aliased))
            },
            cost_estimate=pl.CostEstimate(flops=flops, bytes_accessed=size, transcendentals=0),
            compiler_params=pltpu.CompilerParams(vmem_limit_bytes=VMEM_LIMIT),
        )(
            *(in_hbm(a) for a in fetched),
            *(a if i else in_vmem(a) for a, i in zip(held, integer)),
            *(in_hbm(a) for a in aliased),
        )

    square = HEAD_DIM * HEAD_DIM
    states = (half, HEAD_DIM, HEAD_DIM)
    tokens = (half, tok_rows, HEAD_DIM)
    scalar = (tok_rows, HEAD_DIM)
    unit = 2 * half * tok_rows * square

    def exchange(value):
        return lax.all_to_all(value, "seq", 0, 0, axis_index_groups=chip_groups, tiled=True)

    def spread_sum(pieces):
        return pl.pallas_call(
            spread_sum_kernel,
            in_specs=[VMEM],
            out_specs=VMEM,
            out_shape=jax.ShapeDtypeStruct(pieces.shape, F32),
            compiler_params=pltpu.CompilerParams(vmem_limit_bytes=VMEM_LIMIT),
        )(pieces)

    def sum_over_seq(mine, theirs, beside_sum, beside_gather):
        paired = mine + lax.ppermute(theirs, "seq", swap)
        pieces = exchange(paired.reshape(chips, -1, HEAD_DIM))
        pieces, first = lax.optimization_barrier((pieces, beside_sum()))
        gathered = exchange(spread_sum(pieces)).reshape(states)
        gathered, second = lax.optimization_barrier((gathered, beside_gather(first)))
        return gathered, lax.ppermute(gathered, "seq", swap), first, second

    (theirs,) = call(
        prefix_state_kernel,
        OTHER,
        [prefix_keys, prefix_values],
        [],
        [(states, F32)],
        [],
        unit,
    )
    (mine,) = call(prefix_state_kernel, OWN, [prefix_keys, prefix_values], [], [(states, F32)], [], unit)

    kv_qt = [(states, F32), ((half, HEAD_DIM, tok_rows), BF16)]
    token_parts = [queries, keys, values]

    def intra_other():
        outs = [(tokens, F32), *kv_qt]
        return call(intra_kernel, OTHER, token_parts, [], [], outs, 9 * unit // 2)

    def intra_own(_):
        both = (half, tok_rows + HEAD_DIM, HEAD_DIM)
        outs = [(buffer_shape(both, LARGE), F32)]
        return call(intra_kernel, OWN, token_parts, [], outs, kv_qt[1:], 9 * unit // 2)

    total_own, total_other, (o_other, kv_other, qt_other), (o_own, qt_own) = sum_over_seq(
        mine, theirs, intra_other, intra_own
    )

    def forward(other, streams, held, **options):
        return call(
            forward_kernel,
            other,
            streams,
            held,
            [(tokens, F32), ((2, tok_rows), F32)],
            [((half, 2, HEAD_DIM, HEAD_DIM), BF16)],
            unit,
            scratch=[pltpu.VMEM(scalar, F32)] * 2,
            **options,
        )

    o_own, stats, dy_own, q_other, dy_other, kv_other, o_other, m_own = forward(
        OWN,
        [queries, cotangent],
        [o_own, total_own, gains],
        keep=[1],
        late=[(a, OTHER, LARGE) for a in (queries, cotangent, kv_other, o_other)],
    )
    o_other, stats, m_other = forward(
        OTHER, [], [q_other, dy_other, kv_other, o_other, total_other, gains, stats]
    )
    all_stats = [stats] + [
        lax.ppermute(stats, "head", [(i, (i + k) % head_size) for i in range(head_size)])
        for k in range(1, head_size)
    ]
    qts = call(bring_kernel, OWN, [], [stats], [], [], 0, late=[(qt_own, OWN, LARGE), (qt_other, OTHER, LARGE)])
    all_stats, (qt_own, qt_other) = lax.optimization_barrier((all_stats, qts))

    def state_grad(other, dy, o, qt, scalars):
        first = len(scalars) > 2
        outs = [(states, F32)] + [(scalar, F32), (scalar, F32)] * first
        kernel = functools.partial(state_grad_kernel, first)
        held = [dy, o, gains, qt, *scalars]
        return call(kernel, other, [], held, outs, [(states, BF16)], unit)

    theirs, inv, coef, later_other = state_grad(
        OTHER, dy_other, o_other, qt_other, [lengths, *all_stats]
    )
    mine, later_own = state_grad(OWN, dy_own, o_own, qt_own, [inv, coef])

    def backward(other, o, m, later, before=(), late=()):
        return call(
            backward_kernel,
            other,
            [queries, keys, values, cotangent, o, m, later],
            [gains, inv, coef],
            [],
            [(queries.shape, BF16)] * 4,
            16 * unit,
            group=SMALL,
            aliased=before,
            late=late,
        )

    total_own, total_other, _, (pre_k, *grads) = sum_over_seq(
        mine,
        theirs,
        lambda: backward(OWN, o_own, m_own, later_own),
        lambda before: backward(
            OTHER, o_other, m_other, later_other, before, [(prefix_keys, OWN, LARGE)]
        ),
    )

    def prefix_grad(other, streams, held, **options):
        outs = [(prefix_keys.shape, BF16)] * 2
        return call(prefix_grad_kernel, other, streams, held, [], outs, 4 * unit, **options)

    pre_k, pre_v, *prefix_grads = prefix_grad(
        OWN, [prefix_values], [pre_k, total_own], late=[(a, OTHER, SMALL) for a in (prefix_keys, prefix_values)]
    )
    prefix_grads = prefix_grad(
        OTHER, [], [pre_k, total_other, pre_v], group=SMALL, aliased=prefix_grads
    )
    return (*grads, *prefix_grads)


VMEM_LIMIT = 14 * MIB


def solution(mesh):
    spread = P("seq", "head")
    return jax.shard_map(
        body,
        mesh=mesh,
        in_specs=(spread,) * 6 + (P("head"), P("seq")),
        out_specs=(spread,) * 6,
        check_vma=False,
    )
```

```python
import functools

import jax
import jax.numpy as jnp
from jax import lax
from jax.experimental import pallas as pl
from jax.experimental.pallas import tpu as pltpu
from jax.sharding import PartitionSpec as P

H = 64
HEAD_DIM = 128
BLOCK = 256
WIDTH = H * HEAD_DIM
EPSILON = 1e-06

LARGE, SMALL = 4, 2
MIB = 1024 * 1024

F32 = jnp.float32
BF16 = jnp.bfloat16


def dot_nn(a, b):
    return lax.dot_general(a, b, (((1,), (0,)), ((), ())), preferred_element_type=F32)


def dot_nt(a, b):
    return lax.dot_general(a, b, (((1,), (1,)), ((), ())), preferred_element_type=F32)


def dot_tn(a, b):
    return lax.dot_general(a, b, (((0,), (0,)), ((), ())), preferred_element_type=F32)


def lanes(head):
    return slice(head * HEAD_DIM, (head + 1) * HEAD_DIM)


def rows(block):
    return slice(block * BLOCK, (block + 1) * BLOCK)


def block_mask(upper):
    row = lax.broadcasted_iota(jnp.int32, (BLOCK, BLOCK), 0)
    column = lax.broadcasted_iota(jnp.int32, (BLOCK, BLOCK), 1)
    return column >= row if upper else row >= column


class Slabs:
    def __init__(self, ref, buffers, semaphores, other, out=False):
        core = lax.axis_index("seq") % 2
        self.half = 1 - core if other else core
        self.ref, self.buffers, self.semaphores, self.out = ref, buffers, semaphores, out

    def copy(self, g):
        if len(self.ref.shape) == 2:
            slab = self.buffers.shape[-1]
            start = pl.multiple_of(self.half * (self.buffers.shape[0] * slab) + g * slab, slab)
            there = self.ref.at[:, pl.ds(start, slab)]
        else:
            group = self.buffers.shape[1]
            there = self.ref.at[pl.ds(g * group, group)]
        here = self.buffers.at[g]
        source, target = (here, there) if self.out else (there, here)
        return pltpu.make_async_copy(source, target, self.semaphores.at[g])

    def __getitem__(self, index):
        return self.buffers[index]

    def __setitem__(self, index, value):
        self.buffers[index] = value


def buffer_shape(shape, group):
    if len(shape) == 2:
        slab = group * HEAD_DIM
        return (shape[1] // 2 // slab, shape[0], slab)
    return (shape[0] // group, group) + tuple(shape[1:])


def streamed(kernel, half, group, groups, whole, ins, outs, late, push, rest):
    for copy in whole:
        copy.start()
    for slabs in (ins, push, late):
        for g in range(max([slab.buffers.shape[0] for slab in slabs], default=0)):
            for slab in slabs:
                if g < slab.buffers.shape[0]:
                    slab.copy(g).start()
    steps = kernel(half, group, ins, outs, rest)
    step = next(steps)
    for copy in whole:
        copy.wait()
    for g in range(groups):
        for slab in ins:
            slab.copy(g).wait()
        step(g)
        for slab in outs:
            slab.copy(g).start()
    for _ in steps:
        pass
    for slab in (*outs, *late, *push):
        for g in range(slab.buffers.shape[0]):
            slab.copy(g).wait()


def prefix_state_kernel(half, group, ins, outs, rest):
    k, v, s_ref = (*ins, *rest)

    def step(g):
        for h in range(group):
            s_ref[g * group + h] = dot_tn(k[g, :, lanes(h)], v[g, :, lanes(h)])

    yield step


def bring_kernel(half, group, ins, outs, rest):
    yield lambda g: None


def intra_kernel(half, group, ins, outs, rest):
    o_all, kv_all, qt_all = outs
    lower = block_mask(False)

    def step(g):
        for h in range(group):
            for b in range(2):
                q, k, v = (slab[g, rows(b), lanes(h)] for slab in ins)
                scores = jnp.where(lower, dot_nt(q, k), 0.0).astype(BF16)
                o_all[g, h, rows(b)] = dot_nn(scores, v)
                if b == 0:
                    kv_all[g, h] = dot_tn(k, v)
            qt_all[g, h] = ins[0][g, :, lanes(h)].T

    yield step


def spread_sum_kernel(pieces_ref, out_ref):
    total = jnp.sum(pieces_ref[...], axis=0)
    for i in range(out_ref.shape[0]):
        out_ref[i] = total


def forward_kernel(half, group, ins, outs, rest):
    *operands, o_ref, m_all, stats_ref, square_acc, inner_acc = rest
    q, dy, kv, intra, s_ref, gain_ref, *before = (*ins, *operands)
    heads = o_ref.shape[0]
    square_acc[...] = jnp.zeros_like(square_acc)
    inner_acc[...] = jnp.zeros_like(inner_acc)

    def step(g):
        for b in range(2):
            square = inner = 0.0
            for h in range(group):
                head = g * group + h
                state = s_ref[head] if b == 0 else s_ref[head] + kv[g, h]
                m = state.astype(BF16)
                m_all[g, h, b] = m
                o = intra[g, h, rows(b)] + dot_nn(q[g, rows(b), lanes(h)], m)
                o_ref[head, rows(b)] = o
                gain = gain_ref[half * heads + head]
                square = square + o * o
                inner = inner + gain * dy[g, rows(b), lanes(h)].astype(F32) * o
            square_acc[rows(b)] += square
            inner_acc[rows(b)] += inner

    yield step
    for i, acc in enumerate((square_acc, inner_acc)):
        row = jnp.sum(acc[...].T, axis=0, keepdims=True)
        if before:
            row = row + before[0][i : i + 1]
        stats_ref[i : i + 1] = row


def state_grad_kernel(first, half, group, ins, outs, rest):
    dy_ref, o_ref, gain_ref, qt_ref, *rest = rest
    if first:
        length_ref, *stats, ds_ref, g_all, inv_ref, coef_ref = rest
        total = sum(ref[...] for ref in stats[1:]) + stats[0][...]
        inv = 1.0 / jnp.sqrt(total[0:1] / WIDTH + EPSILON)
        coef = total[1:2] * (inv * inv * inv) / WIDTH
        live = lax.broadcasted_iota(jnp.int32, inv.shape, 1) < length_ref[0]
        for value, ref in ((inv, inv_ref), (coef, coef_ref)):
            value = jnp.where(live, value, 0.0)
            for n in range(value.shape[1] // HEAD_DIM):
                square = jnp.broadcast_to(value[:, lanes(n)], (HEAD_DIM, HEAD_DIM))
                ref[n * HEAD_DIM : (n + 1) * HEAD_DIM] = square.T
    else:
        (g_all,) = outs
        inv_ref, coef_ref, ds_ref = rest
    heads = o_ref.shape[0]

    def step(g):
        for h in range(group):
            head = g * group + h
            scaled = gain_ref[half * heads + head] * dy_ref[g, :, lanes(h)].astype(F32)
            do = (scaled * inv_ref[...] - o_ref[head] * coef_ref[...]).astype(BF16)
            later = dot_nn(qt_ref[g, h, :, rows(1)], do[rows(1)])
            ds_ref[head] = later + dot_nn(qt_ref[g, h, :, rows(0)], do[rows(0)])
            g_all[g, h] = later.astype(BF16)

    yield step


def backward_kernel(half, group, ins, outs, rest):
    q_all, k_all, v_all, dy, o_all, m_all, g_all = ins
    normed, dq_all, dk_all, dv_all = outs
    gain_ref, inv_ref, coef_ref = rest
    heads = gain_ref.shape[0] // 2
    lower, upper = block_mask(False), block_mask(True)

    def step(g):
        for h in range(group):
            o = o_all[g, h]
            gain = gain_ref[half * heads + g * group + h]
            normed[g, :, lanes(h)] = (gain * o * inv_ref[...]).astype(BF16)
            scaled = gain * dy[g, :, lanes(h)].astype(F32)
            do_all = (scaled * inv_ref[...] - o * coef_ref[...]).astype(BF16)
            later = g_all[g, h]
            for b in range(2):
                q, k, v = (slab[g, rows(b), lanes(h)] for slab in (q_all, k_all, v_all))
                do = do_all[rows(b)]
                p = jnp.where(lower, dot_nt(do, v), 0.0).astype(BF16)
                p_t = jnp.where(upper, dot_nt(v, do), 0.0).astype(BF16)
                scores_t = jnp.where(upper, dot_nt(k, q), 0.0).astype(BF16)
                dq = dot_nt(do, m_all[g, h, b]) + dot_nn(p, k)
                dk = dot_nn(p_t, q)
                dv = dot_nn(scores_t, do)
                if b == 0:
                    dk = dk + dot_nt(v, later)
                    dv = dv + dot_nn(k, later)
                for slab, value in ((dq_all, dq), (dk_all, dk), (dv_all, dv)):
                    slab[g, rows(b), lanes(h)] = value.astype(BF16)

    yield step


def prefix_grad_kernel(half, group, ins, outs, rest):
    dk, dv = outs
    k_ref, v_ref, ds_ref = rest

    def step(g):
        for h in range(group):
            ds = ds_ref[g * group + h]
            high = ds.astype(BF16)
            low = (ds - high.astype(F32)).astype(BF16)
            k, v = k_ref[g, :, lanes(h)], v_ref[g, :, lanes(h)]
            dk[g, :, lanes(h)] = dot_nt(
                jnp.concatenate([v, v], 1), jnp.concatenate([high, low], 1)
            ).astype(BF16)
            dv[g, :, lanes(h)] = dot_nn(
                jnp.concatenate([k, k], 1), jnp.concatenate([high, low], 0)
            ).astype(BF16)

    yield step


HBM = pl.BlockSpec(memory_space=pltpu.HBM)
VMEM = pl.BlockSpec(memory_space=pltpu.VMEM)
SMEM = pl.BlockSpec(memory_space=pltpu.SMEM)


def in_hbm(array):
    return pltpu.with_memory_space_constraint(array, pltpu.HBM)


def in_vmem(array):
    return pltpu.with_memory_space_constraint(array, pltpu.VMEM)


def body(queries, keys, values, cotangent, prefix_keys, prefix_values, gain, lengths):
    tok_rows, tok_cols = queries.shape
    half = tok_cols // HEAD_DIM // 2
    seq_size = lax.axis_size("seq")
    head_size = lax.axis_size("head")
    chips = seq_size // 2
    swap = [(i, i ^ 1) for i in range(seq_size)]
    chip_groups = [list(range(c, seq_size, 2)) for c in range(2)]
    gains = gain.reshape(2 * half, 1, HEAD_DIM)
    OWN, OTHER = False, True

    def call(kernel, other, streams, held, outs, out_streams, flops, group=LARGE, scratch=(), aliased=(), late=(), keep=(), whole=(), push=()):
        n_in, n_out, n_late = len(streams), len(out_streams), len(late)
        fetched = [*streams, *(a for a, *_ in late), *whole]
        kept = [pltpu.VMEM(buffer_shape(streams[i].shape, group), streams[i].dtype) for i in keep]
        kept += [pltpu.VMEM(buffer_shape(a.shape, n), a.dtype) for a, _, n in late]
        in_scratch = [i for i in range(n_in) if i not in keep]
        buffers = [
            pltpu.VMEM(buffer_shape(streams[i].shape, group), streams[i].dtype) for i in in_scratch
        ]
        buffers += [pltpu.VMEM(buffer_shape(s, group), d) for s, d in out_streams]
        buffers += [pltpu.VMEM(a.shape, a.dtype) for a in whole]
        results = [pltpu.VMEM(s, d) for s, d in outs] + kept
        results += [pltpu.HBM(s, d) for s, d in out_streams]
        results += [pltpu.HBM(s, a.dtype) for a, s in push]
        n_push = len(push)
        groups = half // group
        size = sum(a.size * a.dtype.itemsize for a in (*fetched, *held))

        def run(*refs):
            refs = list(refs)

            def take(count):
                taken = refs[:count]
                del refs[:count]
                return taken

            sources, late_sources, whole_sources, held_refs, push_buffers, _ = (
                take(n) for n in (n_in, n_late, len(whole), len(held), n_push, len(aliased))
            )
            out_refs, kept_refs, late_buffers, targets, push_targets = (
                take(n) for n in (len(outs), len(keep), n_late, n_out, n_push)
            )
            scratch_refs, loose, out_buffers, whole_refs = (
                take(n) for n in (len(scratch), len(in_scratch), n_out, len(whole))
            )
            (sems,) = refs
            copies = [
                pltpu.make_async_copy(a, b, sems.at[n_in + n_late + n_out + i, 0])
                for i, (a, b) in enumerate(zip(whole_sources, whole_refs))
            ]
            in_buffers = dict(zip(keep, kept_refs)) | dict(zip(in_scratch, loose))
            ins = [Slabs(sources[i], in_buffers[i], sems.at[i], other) for i in range(n_in)]
            brought = [
                Slabs(late_sources[i], late_buffers[i], sems.at[n_in + i], late[i][1])
                for i in range(n_late)
            ]
            written = [
                Slabs(targets[i], out_buffers[i], sems.at[n_in + n_late + i], other, True)
                for i in range(n_out)
            ]
            core = lax.axis_index("seq") % 2
            last = n_in + n_late + n_out + len(whole)
            pushed = [
                Slabs(a, b, sems.at[last + i], other, True)
                for i, (a, b) in enumerate(zip(push_targets, push_buffers))
            ]
            this_half = 1 - core if other else core
            rest = [*held_refs, *whole_refs, *out_refs, *scratch_refs]
            streamed(kernel, this_half, group, groups, copies, ins, written, brought, pushed, rest)

        in_place = [*held, *(a for a, _ in push)]
        integer = [jnp.issubdtype(a.dtype, jnp.integer) for a in in_place]
        first_aliased = len(fetched) + len(in_place)
        return pl.pallas_call(
            run,
            in_specs=[HBM] * len(fetched)
            + [SMEM if i else VMEM for i in integer]
            + [HBM] * len(aliased),
            out_specs=[VMEM] * (len(outs) + len(kept)) + [HBM] * (n_out + n_push),
            out_shape=results,
            scratch_shapes=[
                *scratch,
                *buffers,
                pltpu.SemaphoreType.DMA(
                    (n_in + n_late + n_out + len(whole) + n_push, half // SMALL)
                ),
            ],
            input_output_aliases={
                first_aliased + i: len(outs) + len(kept) + i for i in range(len(aliased))
            },
            cost_estimate=pl.CostEstimate(flops=flops, bytes_accessed=size, transcendentals=0),
            compiler_params=pltpu.CompilerParams(vmem_limit_bytes=VMEM_LIMIT),
        )(
            *(in_hbm(a) for a in fetched),
            *(a if i else in_vmem(a) for a, i in zip(in_place, integer)),
            *(in_hbm(a) for a in aliased),
        )

    square = HEAD_DIM * HEAD_DIM
    states = (half, HEAD_DIM, HEAD_DIM)
    tokens = (half, tok_rows, HEAD_DIM)
    scalar = (tok_rows, HEAD_DIM)
    unit = 2 * half * tok_rows * square

    def exchange(value):
        return lax.all_to_all(value, "seq", 0, 0, axis_index_groups=chip_groups, tiled=True)

    def spread_sum(pieces):
        return pl.pallas_call(
            spread_sum_kernel,
            in_specs=[VMEM],
            out_specs=VMEM,
            out_shape=jax.ShapeDtypeStruct(pieces.shape, F32),
            compiler_params=pltpu.CompilerParams(vmem_limit_bytes=VMEM_LIMIT),
        )(pieces)

    def sum_over_seq(mine, theirs, beside_sum, beside_gather):
        paired = mine + lax.ppermute(theirs, "seq", swap)
        pieces = exchange(paired.reshape(chips, -1, HEAD_DIM))
        pieces, first = lax.optimization_barrier((pieces, beside_sum()))
        gathered = exchange(spread_sum(pieces)).reshape(states)
        gathered, second = lax.optimization_barrier((gathered, beside_gather(first)))
        return gathered, lax.ppermute(gathered, "seq", swap), first, second

    (theirs,) = call(
        prefix_state_kernel,
        OTHER,
        [prefix_keys, prefix_values],
        [],
        [(states, F32)],
        [],
        unit,
    )
    (mine,) = call(prefix_state_kernel, OWN, [prefix_keys, prefix_values], [], [(states, F32)], [], unit)

    token_parts = [queries, keys, values]

    def intra(other):
        outs = [(tokens, F32), (states, F32), ((half, HEAD_DIM, tok_rows), BF16)]
        return call(intra_kernel, other, token_parts, [], [], outs, 9 * unit // 2)

    total_own, total_other, (o_own, kv_own, qt_own), (o_other, kv_other, qt_other) = sum_over_seq(
        mine, theirs, lambda: intra(OWN), lambda _: intra(OTHER)
    )

    rounded = (half, 2, HEAD_DIM, HEAD_DIM)

    def forward(other, streams, held, **options):
        return call(
            forward_kernel,
            other,
            streams,
            held,
            [(tokens, F32), (buffer_shape(rounded, LARGE), BF16), ((2, tok_rows), F32)],
            [],
            unit,
            scratch=[pltpu.VMEM(scalar, F32)] * 2,
            **options,
        )

    o_own, m_own, stats, dy_own, q_other, dy_other, kv_other, o_other = forward(
        OWN,
        [queries, cotangent, kv_own, o_own],
        [total_own, gains],
        keep=[1],
        late=[(a, OTHER, LARGE) for a in (queries, cotangent, kv_other, o_other)],
    )
    o_other, m_other, stats = forward(
        OTHER, [], [q_other, dy_other, kv_other, o_other, total_other, gains, stats]
    )
    all_stats = [stats] + [
        lax.ppermute(stats, "head", [(i, (i + k) % head_size) for i in range(head_size)])
        for k in range(1, head_size)
    ]
    qts = call(
        bring_kernel,
        OWN,
        [],
        [stats],
        [],
        [],
        0,
        late=[(qt_own, OWN, LARGE), (qt_other, OTHER, LARGE)],
        push=[(m_own, rounded), (m_other, rounded)],
    )
    all_stats, (qt_own, qt_other, m_own, m_other) = lax.optimization_barrier((all_stats, qts))

    def state_grad(other, dy, o, qt, scalars, **options):
        first = len(scalars) > 2
        outs, out_streams = [(states, F32)], [(states, BF16)]
        if first:
            outs += [(buffer_shape(states, LARGE), BF16), (scalar, F32), (scalar, F32)]
            out_streams = []
        kernel = functools.partial(state_grad_kernel, first)
        held = [dy, o, gains, qt, *scalars]
        return call(kernel, other, [], held, outs, out_streams, unit, **options)

    theirs, later_other, inv, coef = state_grad(
        OTHER, dy_other, o_other, qt_other, [lengths, *all_stats]
    )
    mine, later_own, later_other = state_grad(
        OWN, dy_own, o_own, qt_own, [inv, coef], push=[(later_other, states)]
    )

    def backward(other, o, m, later, before=(), late=()):
        return call(
            backward_kernel,
            other,
            [queries, keys, values, cotangent, o, m, later],
            [gains],
            [],
            [(queries.shape, BF16)] * 4,
            16 * unit,
            whole=[inv, coef],
            group=SMALL,
            aliased=before,
            late=late,
        )

    total_own, total_other, _, (pre_k, pre_v, *grads) = sum_over_seq(
        mine,
        theirs,
        lambda: backward(OWN, o_own, m_own, later_own),
        lambda before: backward(
            OTHER, o_other, m_other, later_other, before, [(prefix_keys, OWN, LARGE), (prefix_values, OWN, LARGE)]
        ),
    )

    def prefix_grad(other, k, v, total, **options):
        outs = [(prefix_keys.shape, BF16)] * 2
        return call(prefix_grad_kernel, other, [], [k, v, total], [], outs, 4 * unit, **options)

    pre_k, pre_v, *prefix_grads = prefix_grad(
        OWN, pre_k, pre_v, total_own, late=[(a, OTHER, SMALL) for a in (prefix_keys, prefix_values)]
    )
    prefix_grads = prefix_grad(
        OTHER, pre_k, pre_v, total_other, group=SMALL, aliased=prefix_grads
    )
    return (*grads, *prefix_grads)


VMEM_LIMIT = 14 * MIB


def solution(mesh):
    spread = P("seq", "head")
    return jax.shard_map(
        body,
        mesh=mesh,
        in_specs=(spread,) * 6 + (P("head"), P("seq")),
        out_specs=(spread,) * 6,
        check_vma=False,
    )
```

```python
import functools

import jax
import jax.numpy as jnp
from jax import lax
from jax.experimental import pallas as pl
from jax.experimental.pallas import tpu as pltpu
from jax.sharding import PartitionSpec as P

H = 64
HEAD_DIM = 128
BLOCK = 256
WIDTH = H * HEAD_DIM
EPSILON = 1e-06

LARGE, SMALL = 4, 2
MIB = 1024 * 1024

F32 = jnp.float32
BF16 = jnp.bfloat16


def dot_nn(a, b):
    return lax.dot_general(a, b, (((1,), (0,)), ((), ())), preferred_element_type=F32)


def dot_nt(a, b):
    return lax.dot_general(a, b, (((1,), (1,)), ((), ())), preferred_element_type=F32)


def dot_tn(a, b):
    return lax.dot_general(a, b, (((0,), (0,)), ((), ())), preferred_element_type=F32)


def lanes(head):
    return slice(head * HEAD_DIM, (head + 1) * HEAD_DIM)


def rows(block):
    return slice(block * BLOCK, (block + 1) * BLOCK)


def block_mask(upper):
    row = lax.broadcasted_iota(jnp.int32, (BLOCK, BLOCK), 0)
    column = lax.broadcasted_iota(jnp.int32, (BLOCK, BLOCK), 1)
    return column >= row if upper else row >= column


class Slabs:
    def __init__(self, ref, buffers, semaphores, other, out=False):
        core = lax.axis_index("seq") % 2
        self.half = 1 - core if other else core
        self.ref, self.buffers, self.semaphores, self.out = ref, buffers, semaphores, out

    def copy(self, g):
        if len(self.ref.shape) == 2:
            slab = self.buffers.shape[-1]
            start = pl.multiple_of(self.half * (self.buffers.shape[0] * slab) + g * slab, slab)
            there = self.ref.at[:, pl.ds(start, slab)]
        else:
            group = self.buffers.shape[1]
            there = self.ref.at[pl.ds(g * group, group)]
        here = self.buffers.at[g]
        source, target = (here, there) if self.out else (there, here)
        return pltpu.make_async_copy(source, target, self.semaphores.at[g])

    def __getitem__(self, index):
        return self.buffers[index]

    def __setitem__(self, index, value):
        self.buffers[index] = value


def buffer_shape(shape, group):
    if len(shape) == 2:
        slab = group * HEAD_DIM
        return (shape[1] // 2 // slab, shape[0], slab)
    return (shape[0] // group, group) + tuple(shape[1:])


def streamed(kernel, half, group, groups, whole, ins, outs, late, push, rest):
    for copy in whole:
        copy.start()
    for slabs in (ins, push, late):
        for g in range(max([slab.buffers.shape[0] for slab in slabs], default=0)):
            for slab in slabs:
                if g < slab.buffers.shape[0]:
                    slab.copy(g).start()
    steps = kernel(half, group, ins, outs, rest)
    step = next(steps)
    for copy in whole:
        copy.wait()
    for g in range(groups):
        for slab in ins:
            slab.copy(g).wait()
        step(g)
        for slab in outs:
            slab.copy(g).start()
    for _ in steps:
        pass
    for slab in (*outs, *late, *push):
        for g in range(slab.buffers.shape[0]):
            slab.copy(g).wait()


def prefix_state_kernel(half, group, ins, outs, rest):
    k, v, s_ref = (*ins, *rest)

    def step(g):
        for h in range(group):
            s_ref[g * group + h] = dot_tn(k[g, :, lanes(h)], v[g, :, lanes(h)])

    yield step


def bring_kernel(half, group, ins, outs, rest):
    yield lambda g: None


def intra_kernel(half, group, ins, outs, rest):
    o_all, kv_all, qt_all = outs
    lower = block_mask(False)

    def step(g):
        for h in range(group):
            for b in range(2):
                q, k, v = (slab[g, rows(b), lanes(h)] for slab in ins)
                scores = jnp.where(lower, dot_nt(q, k), 0.0).astype(BF16)
                o_all[g, h, rows(b)] = dot_nn(scores, v)
                if b == 0:
                    kv_all[g, h] = dot_tn(k, v)
            qt_all[g, h] = ins[0][g, :, lanes(h)].T

    yield step


def spread_sum_kernel(pieces_ref, out_ref):
    total = jnp.sum(pieces_ref[...], axis=0)
    for i in range(out_ref.shape[0]):
        out_ref[i] = total


def forward_kernel(half, group, ins, outs, rest):
    *operands, o_ref, m_all, stats_ref, square_acc, inner_acc = rest
    q, dy, kv, intra, s_ref, gain_ref, *before = (*ins, *operands)
    heads = o_ref.shape[0]
    square_acc[...] = jnp.zeros_like(square_acc)
    inner_acc[...] = jnp.zeros_like(inner_acc)

    def step(g):
        for b in range(2):
            square = inner = 0.0
            for h in range(group):
                head = g * group + h
                state = s_ref[head] if b == 0 else s_ref[head] + kv[g, h]
                m = state.astype(BF16)
                m_all[g, h, b] = m
                o = intra[g, h, rows(b)] + dot_nn(q[g, rows(b), lanes(h)], m)
                o_ref[head, rows(b)] = o
                gain = gain_ref[half * heads + head]
                square = square + o * o
                inner = inner + gain * dy[g, rows(b), lanes(h)].astype(F32) * o
            square_acc[rows(b)] += square
            inner_acc[rows(b)] += inner

    yield step
    for i, acc in enumerate((square_acc, inner_acc)):
        row = jnp.sum(acc[...].T, axis=0, keepdims=True)
        if before:
            row = row + before[0][i : i + 1]
        stats_ref[i : i + 1] = row


def state_grad_kernel(first, half, group, ins, outs, rest):
    dy_ref, o_ref, gain_ref, qt_ref, *rest = rest
    if first:
        length_ref, *stats, ds_ref, g_all, inv_ref, coef_ref = rest
        total = sum(ref[...] for ref in stats[1:]) + stats[0][...]
        inv = 1.0 / jnp.sqrt(total[0:1] / WIDTH + EPSILON)
        coef = total[1:2] * (inv * inv * inv) / WIDTH
        live = lax.broadcasted_iota(jnp.int32, inv.shape, 1) < length_ref[0]
        for value, ref in ((inv, inv_ref), (coef, coef_ref)):
            value = jnp.where(live, value, 0.0)
            for n in range(value.shape[1] // HEAD_DIM):
                square = jnp.broadcast_to(value[:, lanes(n)], (HEAD_DIM, HEAD_DIM))
                ref[n * HEAD_DIM : (n + 1) * HEAD_DIM] = square.T
    else:
        inv_ref, coef_ref, ds_ref, g_all = rest
    heads = o_ref.shape[0]

    def step(g):
        for h in range(group):
            head = g * group + h
            scaled = gain_ref[half * heads + head] * dy_ref[g, :, lanes(h)].astype(F32)
            do = (scaled * inv_ref[...] - o_ref[head] * coef_ref[...]).astype(BF16)
            later = dot_nn(qt_ref[g, h, :, rows(1)], do[rows(1)])
            ds_ref[head] = later + dot_nn(qt_ref[g, h, :, rows(0)], do[rows(0)])
            g_all[g, h] = later.astype(BF16)

    yield step


def backward_kernel(half, group, ins, outs, rest):
    q_all, k_all, v_all, dy, o_all, m_all, *g_all = ins
    normed, dq_all, dk_all, dv_all = outs
    gain_ref, *held_g, inv_ref, coef_ref = rest
    heads = gain_ref.shape[0] // 2
    lower, upper = block_mask(False), block_mask(True)

    def step(g):
        for h in range(group):
            o = o_all[g, h]
            gain = gain_ref[half * heads + g * group + h]
            normed[g, :, lanes(h)] = (gain * o * inv_ref[...]).astype(BF16)
            scaled = gain * dy[g, :, lanes(h)].astype(F32)
            do_all = (scaled * inv_ref[...] - o * coef_ref[...]).astype(BF16)
            if held_g:
                many = held_g[0].shape[1]
                later = held_g[0][(g * group + h) // many, (g * group + h) % many]
            else:
                later = g_all[0][g, h]
            for b in range(2):
                q, k, v = (slab[g, rows(b), lanes(h)] for slab in (q_all, k_all, v_all))
                do = do_all[rows(b)]
                p = jnp.where(lower, dot_nt(do, v), 0.0).astype(BF16)
                p_t = jnp.where(upper, dot_nt(v, do), 0.0).astype(BF16)
                scores_t = jnp.where(upper, dot_nt(k, q), 0.0).astype(BF16)
                dq = dot_nt(do, m_all[g, h, b]) + dot_nn(p, k)
                dk = dot_nn(p_t, q)
                dv = dot_nn(scores_t, do)
                if b == 0:
                    dk = dk + dot_nt(v, later)
                    dv = dv + dot_nn(k, later)
                for slab, value in ((dq_all, dq), (dk_all, dk), (dv_all, dv)):
                    slab[g, rows(b), lanes(h)] = value.astype(BF16)

    yield step


def prefix_grad_kernel(half, group, ins, outs, rest):
    dk, dv = outs
    k_ref, v_ref, ds_ref = rest

    def step(g):
        for h in range(group):
            ds = ds_ref[g * group + h]
            high = ds.astype(BF16)
            low = (ds - high.astype(F32)).astype(BF16)
            k, v = k_ref[g, :, lanes(h)], v_ref[g, :, lanes(h)]
            dk[g, :, lanes(h)] = dot_nt(
                jnp.concatenate([v, v], 1), jnp.concatenate([high, low], 1)
            ).astype(BF16)
            dv[g, :, lanes(h)] = dot_nn(
                jnp.concatenate([k, k], 1), jnp.concatenate([high, low], 0)
            ).astype(BF16)

    yield step


HBM = pl.BlockSpec(memory_space=pltpu.HBM)
VMEM = pl.BlockSpec(memory_space=pltpu.VMEM)
SMEM = pl.BlockSpec(memory_space=pltpu.SMEM)


def in_hbm(array):
    return pltpu.with_memory_space_constraint(array, pltpu.HBM)


def in_vmem(array):
    return pltpu.with_memory_space_constraint(array, pltpu.VMEM)


def body(queries, keys, values, cotangent, prefix_keys, prefix_values, gain, lengths):
    tok_rows, tok_cols = queries.shape
    half = tok_cols // HEAD_DIM // 2
    seq_size = lax.axis_size("seq")
    head_size = lax.axis_size("head")
    chips = seq_size // 2
    swap = [(i, i ^ 1) for i in range(seq_size)]
    chip_groups = [list(range(c, seq_size, 2)) for c in range(2)]
    gains = gain.reshape(2 * half, 1, HEAD_DIM)
    OWN, OTHER = False, True

    def call(kernel, other, streams, held, outs, out_streams, flops, group=LARGE, scratch=(), aliased=(), late=(), keep=(), whole=(), push=()):
        n_in, n_out, n_late = len(streams), len(out_streams), len(late)
        fetched = [*streams, *(a for a, *_ in late), *whole]
        kept = [pltpu.VMEM(buffer_shape(streams[i].shape, group), streams[i].dtype) for i in keep]
        kept += [pltpu.VMEM(buffer_shape(a.shape, n), a.dtype) for a, _, n in late]
        in_scratch = [i for i in range(n_in) if i not in keep]
        buffers = [
            pltpu.VMEM(buffer_shape(streams[i].shape, group), streams[i].dtype) for i in in_scratch
        ]
        buffers += [pltpu.VMEM(buffer_shape(s, group), d) for s, d in out_streams]
        buffers += [pltpu.VMEM(a.shape, a.dtype) for a in whole]
        results = [pltpu.VMEM(s, d) for s, d in outs] + kept
        results += [pltpu.HBM(s, d) for s, d in out_streams]
        results += [pltpu.HBM(s, a.dtype) for a, s in push]
        n_push = len(push)
        groups = half // group
        size = sum(a.size * a.dtype.itemsize for a in (*fetched, *held))

        def run(*refs):
            refs = list(refs)

            def take(count):
                taken = refs[:count]
                del refs[:count]
                return taken

            sources, late_sources, whole_sources, held_refs, push_buffers, _ = (
                take(n) for n in (n_in, n_late, len(whole), len(held), n_push, len(aliased))
            )
            out_refs, kept_refs, late_buffers, targets, push_targets = (
                take(n) for n in (len(outs), len(keep), n_late, n_out, n_push)
            )
            scratch_refs, loose, out_buffers, whole_refs = (
                take(n) for n in (len(scratch), len(in_scratch), n_out, len(whole))
            )
            (sems,) = refs
            copies = [
                pltpu.make_async_copy(a, b, sems.at[n_in + n_late + n_out + i, 0])
                for i, (a, b) in enumerate(zip(whole_sources, whole_refs))
            ]
            in_buffers = dict(zip(keep, kept_refs)) | dict(zip(in_scratch, loose))
            ins = [Slabs(sources[i], in_buffers[i], sems.at[i], other) for i in range(n_in)]
            brought = [
                Slabs(late_sources[i], late_buffers[i], sems.at[n_in + i], late[i][1])
                for i in range(n_late)
            ]
            written = [
                Slabs(targets[i], out_buffers[i], sems.at[n_in + n_late + i], other, True)
                for i in range(n_out)
            ]
            core = lax.axis_index("seq") % 2
            last = n_in + n_late + n_out + len(whole)
            pushed = [
                Slabs(a, b, sems.at[last + i], other, True)
                for i, (a, b) in enumerate(zip(push_targets, push_buffers))
            ]
            this_half = 1 - core if other else core
            rest = [*held_refs, *whole_refs, *out_refs, *scratch_refs]
            streamed(kernel, this_half, group, groups, copies, ins, written, brought, pushed, rest)

        in_place = [*held, *(a for a, _ in push)]
        integer = [jnp.issubdtype(a.dtype, jnp.integer) for a in in_place]
        first_aliased = len(fetched) + len(in_place)
        return pl.pallas_call(
            run,
            in_specs=[HBM] * len(fetched)
            + [SMEM if i else VMEM for i in integer]
            + [HBM] * len(aliased),
            out_specs=[VMEM] * (len(outs) + len(kept)) + [HBM] * (n_out + n_push),
            out_shape=results,
            scratch_shapes=[
                *scratch,
                *buffers,
                pltpu.SemaphoreType.DMA(
                    (n_in + n_late + n_out + len(whole) + n_push, half // SMALL)
                ),
            ],
            input_output_aliases={
                first_aliased + i: len(outs) + len(kept) + i for i in range(len(aliased))
            },
            cost_estimate=pl.CostEstimate(flops=flops, bytes_accessed=size, transcendentals=0),
            compiler_params=pltpu.CompilerParams(vmem_limit_bytes=VMEM_LIMIT),
        )(
            *(in_hbm(a) for a in fetched),
            *(a if i else in_vmem(a) for a, i in zip(in_place, integer)),
            *(in_hbm(a) for a in aliased),
        )

    square = HEAD_DIM * HEAD_DIM
    states = (half, HEAD_DIM, HEAD_DIM)
    tokens = (half, tok_rows, HEAD_DIM)
    scalar = (tok_rows, HEAD_DIM)
    unit = 2 * half * tok_rows * square

    def exchange(value):
        return lax.all_to_all(value, "seq", 0, 0, axis_index_groups=chip_groups, tiled=True)

    def spread_sum(pieces):
        return pl.pallas_call(
            spread_sum_kernel,
            in_specs=[VMEM],
            out_specs=VMEM,
            out_shape=jax.ShapeDtypeStruct(pieces.shape, F32),
            compiler_params=pltpu.CompilerParams(vmem_limit_bytes=VMEM_LIMIT),
        )(pieces)

    def sum_over_seq(mine, theirs, beside_sum, beside_gather):
        paired = mine + lax.ppermute(theirs, "seq", swap)
        pieces = exchange(paired.reshape(chips, -1, HEAD_DIM))
        pieces, first = lax.optimization_barrier((pieces, beside_sum()))
        gathered = exchange(spread_sum(pieces)).reshape(states)
        gathered, second = lax.optimization_barrier((gathered, beside_gather(first)))
        return gathered, lax.ppermute(gathered, "seq", swap), first, second

    (theirs,) = call(
        prefix_state_kernel,
        OTHER,
        [prefix_keys, prefix_values],
        [],
        [(states, F32)],
        [],
        unit,
    )
    (mine,) = call(prefix_state_kernel, OWN, [prefix_keys, prefix_values], [], [(states, F32)], [], unit)

    token_parts = [queries, keys, values]

    def intra(other):
        outs = [(tokens, F32), (states, F32), ((half, HEAD_DIM, tok_rows), BF16)]
        return call(intra_kernel, other, token_parts, [], [], outs, 9 * unit // 2)

    total_own, total_other, (o_own, kv_own, qt_own), (o_other, kv_other, qt_other) = sum_over_seq(
        mine, theirs, lambda: intra(OWN), lambda _: intra(OTHER)
    )

    rounded = (half, 2, HEAD_DIM, HEAD_DIM)

    def forward(other, streams, held, **options):
        return call(
            forward_kernel,
            other,
            streams,
            held,
            [(tokens, F32), (buffer_shape(rounded, LARGE), BF16), ((2, tok_rows), F32)],
            [],
            unit,
            scratch=[pltpu.VMEM(scalar, F32)] * 2,
            **options,
        )

    o_own, m_own, stats, dy_own, q_other, dy_other, kv_other, o_other = forward(
        OWN,
        [queries, cotangent, kv_own, o_own],
        [total_own, gains],
        keep=[1],
        late=[(a, OTHER, LARGE) for a in (queries, cotangent, kv_other, o_other)],
    )
    o_other, m_other, stats = forward(
        OTHER, [], [q_other, dy_other, kv_other, o_other, total_other, gains, stats]
    )
    all_stats = [stats] + [
        lax.ppermute(stats, "head", [(i, (i + k) % head_size) for i in range(head_size)])
        for k in range(1, head_size)
    ]
    qts = call(
        bring_kernel,
        OWN,
        [],
        [stats],
        [],
        [],
        0,
        late=[(qt_own, OWN, LARGE), (qt_other, OTHER, LARGE)],
        push=[(m_own, rounded), (m_other, rounded)],
    )
    all_stats, (qt_own, qt_other, m_own, m_other) = lax.optimization_barrier((all_stats, qts))

    def state_grad(other, dy, o, qt, scalars, **options):
        first = len(scalars) > 2
        outs = [(states, F32), (buffer_shape(states, LARGE), BF16)]
        outs += [(scalar, F32), (scalar, F32)] * first
        kernel = functools.partial(state_grad_kernel, first)
        held = [dy, o, gains, qt, *scalars]
        return call(kernel, other, [], held, outs, [], unit, **options)

    theirs, later_other, inv, coef = state_grad(
        OTHER, dy_other, o_other, qt_other, [lengths, *all_stats]
    )
    mine, later_own = state_grad(OWN, dy_own, o_own, qt_own, [inv, coef])

    def backward(other, o, m, streams, held, before=(), **options):
        return call(
            backward_kernel,
            other,
            [queries, keys, values, cotangent, o, m, *streams],
            [gains, *held],
            [],
            [(queries.shape, BF16)] * 4,
            16 * unit,
            whole=[inv, coef],
            group=SMALL,
            aliased=before,
            **options,
        )

    total_own, total_other, _, (pre_k, pre_v, *grads) = sum_over_seq(
        mine,
        theirs,
        lambda: backward(OWN, o_own, m_own, [], [later_own], push=[(later_other, states)]),
        lambda before: backward(
            OTHER,
            o_other,
            m_other,
            [before[-1]],
            [],
            before[:-1],
            late=[(prefix_keys, OWN, LARGE), (prefix_values, OWN, LARGE)],
        ),
    )

    def prefix_grad(other, k, v, total, **options):
        outs = [(prefix_keys.shape, BF16)] * 2
        return call(prefix_grad_kernel, other, [], [k, v, total], [], outs, 4 * unit, **options)

    pre_k, pre_v, *prefix_grads = prefix_grad(
        OWN, pre_k, pre_v, total_own, late=[(a, OTHER, SMALL) for a in (prefix_keys, prefix_values)]
    )
    prefix_grads = prefix_grad(
        OTHER, pre_k, pre_v, total_other, group=SMALL, aliased=prefix_grads
    )
    return (*grads, *prefix_grads)


VMEM_LIMIT = 14 * MIB


def solution(mesh):
    spread = P("seq", "head")
    return jax.shard_map(
        body,
        mesh=mesh,
        in_specs=(spread,) * 6 + (P("head"), P("seq")),
        out_specs=(spread,) * 6,
        check_vma=False,
    )
```
